128 devices in a mesh: dp: 16 (over z, y), tensor: 8 (over x, core).
Axes of the slice: x: 4, y: 4, z: 4, core: 2. Of those that a mesh axis runs over, the one named last changes fastest.
Arguments:
- hidden_in: bfloat16 [16, 1024, 1024], P('dp', 'tensor'), may hold values from -6 to 6
- first_gain: bfloat16 [1024], replicated, may hold values from 0.5 to 1.5
- first_shift: bfloat16 [1024], replicated, may hold values from -1 to 1
- second_gain: bfloat16 [1024], replicated, may hold values from 0.5 to 1.5
- second_shift: bfloat16 [1024], replicated, may hold values from -1 to 1
- qkv_weight: bfloat16 [3, 1024, 1024], P(None, None, 'tensor'), may hold values from -0.1875 to 0.1875
- qkv_bias: bfloat16 [3, 1024], P(None, 'tensor'), may hold values from -1 to 1
- dense_weight: bfloat16 [1024, 1024], P('tensor'), may hold values from -3 to 3
- up_weight: bfloat16 [1024, 4096], P(None, 'tensor'), may hold values from -0.1875 to 0.1875
- up_bias: bfloat16 [4096], P('tensor'), may hold values from -1 to 1
- down_weight: bfloat16 [4096, 1024], P('tensor'), may hold values from -0.09375 to 0.09375
- out_bias: bfloat16 [1024], replicated, may hold values from -2.5 to 2.5
- segments: int32 [16, 1024], P('dp'), may hold values from 0 to 2, as said below
- positions: int32 [16, 1024], P('dp'), may hold values from 0 to 1023, as said below
- cotangent: bfloat16 [16, 1024, 1024], P('dp', 'tensor'), may hold values from -6 to 6
Outputs:
- activations: bfloat16 [16, 1024, 1024], P('dp', 'tensor')
- input_grad: float32 [16, 1024, 1024], P('dp', 'tensor')
- qkv_weight_grad: float32 [3, 1024, 1024], P(None, None, 'tensor')
- qkv_bias_grad: float32 [3, 1024], P(None, 'tensor')
- dense_weight_grad: float32 [1024, 1024], P('tensor')
- up_weight_grad: float32 [1024, 4096], P(None, 'tensor')
- up_bias_grad: float32 [4096], P('tensor')
- down_weight_grad: float32 [4096, 1024], P('tensor')
- out_bias_grad: float32 [1024], replicated
- first_gain_grad: float32 [1024], replicated
- first_shift_grad: float32 [1024], replicated
- second_gain_grad: float32 [1024], replicated
- second_shift_grad: float32 [1024], replicated
The draws below stay inside these ranges and needn't reach their ends.
Inputs may be any that keep to these rules, and one draw needn't show every extreme that they name: Segment numbers never fall along a sequence, and every sequence holds segments 0, 1 and 2. `positions`: within a segment the position rises by one from token to token; segments 1 and 2 start at 0, and segment 0 ends at 1023.
All inputs are finite; a program needn't handle non-finite values.
Results may differ from the reference program's by a relative error of at most 0.012.
Values may be sent and summed in bfloat16 or wider, within the bound.
A program may use at most 128 MiB of HBM per device.

```python
import jax
import jax.numpy as jnp
from jax import lax

D = 1024
HEADS = 16
HEAD_DIM = 64
ROT = 16
FF = 4096
SEQ = 1024
SEQUENCES = 16


def document_cuts(key):
    first_key, second_key = jax.random.split(key)
    reach_span = max(SEQ // 16, 2)
    head_cut = jax.random.randint(first_key, (SEQUENCES, 1), 1, reach_span)
    tail_cut = SEQ - jax.random.randint(second_key, (SEQUENCES, 1), 1, reach_span)
    places = jnp.arange(SEQ, dtype=jnp.int32)[None, :]
    return (head_cut.astype(jnp.int32), tail_cut.astype(jnp.int32), places)


def draw_segments(key, part):
    head_cut, tail_cut, places = document_cuts(key)
    return (places >= head_cut).astype(jnp.int32) + (places >= tail_cut).astype(jnp.int32)


def draw_positions(key, part):
    head_cut, tail_cut, places = document_cuts(key)
    inside = jnp.where(places < tail_cut, places - head_cut, places - tail_cut)
    return jnp.where(places < head_cut, places + SEQ - head_cut, inside).astype(jnp.int32)


def levels(rng, shape, cuts, least, top_value):
    gain = 1.0
    for position, parts in cuts:
        draws = jax.random.uniform(jax.random.fold_in(jax.random.fold_in(rng, 6), position), (parts,), jnp.float32, least / len(cuts), top_value / len(cuts))
        gain = gain * jnp.repeat(jnp.exp(draws), shape[position] // parts).reshape((-1,) + (1,) * (len(shape) - 1 - position))
    return gain


def gaussian(own_key, shape, deviation, limit, cuts=(), kind=jnp.bfloat16):
    values = deviation * jax.random.normal(own_key, shape, jnp.float32)
    if cuts:
        values = values * levels(own_key, shape, cuts, -0.22, 0.18)
    return jnp.clip(values, -limit, limit).astype(kind)


def setup_inputs(seed: int = 0) -> dict:
    arg_keys = jax.random.split(jax.random.key(seed), 16)
    return {
        "hidden_in": gaussian(arg_keys[0], (SEQUENCES, SEQ, D), 1.0, 6.0, ((0, 16), (1, 8))),
        "first_gain": jnp.clip(1.0 + 0.1 * jax.random.normal(arg_keys[1], (D,), jnp.float32), 0.5, 1.5).astype(jnp.bfloat16),
        "first_shift": gaussian(arg_keys[2], (D,), 0.2, 1.0),
        "second_gain": jnp.clip(1.0 + 0.1 * jax.random.normal(arg_keys[3], (D,), jnp.float32), 0.5, 1.5).astype(jnp.bfloat16),
        "second_shift": gaussian(arg_keys[4], (D,), 0.2, 1.0),
        "qkv_weight": gaussian(arg_keys[5], (3, D, D), D ** -0.5, 0.1875, ((2, 8),)),
        "qkv_bias": gaussian(arg_keys[6], (3, D), 0.2, 1.0, ((1, 8),)),
        "dense_weight": gaussian(arg_keys[7], (D, D), (max(D // 256, 1)) ** -0.5, 3.0, ((0, 8),)),
        "up_weight": gaussian(arg_keys[8], (D, FF), D ** -0.5, 0.1875, ((1, 8),)),
        "up_bias": gaussian(arg_keys[9], (FF,), 0.2, 1.0, ((0, 8),)),
        "down_weight": gaussian(arg_keys[10], (FF, D), FF ** -0.5, 0.09375, ((0, 8),)),
        "out_bias": gaussian(arg_keys[11], (D,), 0.5, 2.5),
        "segments": draw_segments(jax.random.fold_in(arg_keys[15], 71), 0),
        "positions": draw_positions(jax.random.fold_in(arg_keys[15], 71), 0),
        "cotangent": gaussian(arg_keys[14], (SEQUENCES, SEQ, D), 1.0, 6.0, ((0, 16), (1, 8))),
    }


norm_epsilon = 1e-05

@jax.custom_vjp
def low(v):
    return lax.optimization_barrier(v.astype(jnp.bfloat16)).astype(jnp.float32)

@jax.custom_vjp
def low_back(v):
    return v

def low_keep(v):
    return (low(v), None)

def low_pass(kept, grad):
    return (grad,)

def back_keep(v):
    return (v, None)

def back_low(kept, grad):
    return (low(grad),)
low.defvjp(low_keep, low_pass)
low_back.defvjp(back_keep, back_low)

def matmul(left, right):
    return jnp.dot(left, right, precision=lax.Precision.HIGHEST, preferred_element_type=jnp.float32)

def layer_norm(values, norm_gain, norm_shift):
    mean_value = lax.optimization_barrier(jnp.mean(values, axis=-1, keepdims=True))
    centered = values - mean_value
    spread = lax.optimization_barrier(jnp.mean(centered * centered, axis=-1, keepdims=True))
    return centered * lax.rsqrt(spread + norm_epsilon) * norm_gain + norm_shift

def angles(positions):
    half_rot = ROT // 2
    frequency = 10000.0 ** (-2.0 * jnp.arange(half_rot, dtype=jnp.float32) / ROT)
    phase_angle = positions.astype(jnp.float32)[..., None] * frequency
    return (jnp.cos(phase_angle), jnp.sin(phase_angle))

def rotate(values, cos_table, sine_table):
    half_rot = cos_table.shape[-1]
    first_half = values[..., :half_rot]
    second_half = values[..., half_rot:2 * half_rot]
    cos_heads = cos_table[..., None, :]
    sin_heads = sine_table[..., None, :]
    return jnp.concatenate([first_half * cos_heads - second_half * sin_heads, second_half * cos_heads + first_half * sin_heads, values[..., 2 * half_rot:]], axis=-1)

def allowed_keys(segment_row, first_query, query_count):
    query_place = first_query + jnp.arange(query_count, dtype=jnp.int32)
    key_place = jnp.arange(segment_row.shape[0], dtype=jnp.int32)
    query_segment = lax.dynamic_slice_in_dim(segment_row, first_query, query_count, 0)
    return (key_place[None, :] <= query_place[:, None]) & (segment_row[None, :] == query_segment[:, None])

def split_heads(values):
    return values.reshape(SEQ, HEADS, HEAD_DIM)

def one_layer(parameters, seq_rows, segment_row, position_row):
    gain_one, shift_one, gain_two, shift_two, qkv_full, qkv_shift, dense_full, up_full, up_shift, down_full, out_shift = parameters
    normed_one = low(layer_norm(seq_rows, gain_one, shift_one))
    normed_two = low(layer_norm(seq_rows, gain_two, shift_two))
    cos_table, sine_table = angles(position_row)
    query_pre = split_heads(low_back(matmul(normed_one, qkv_full[0]) + qkv_shift[0]))
    key_pre = split_heads(low_back(matmul(normed_one, qkv_full[1]) + qkv_shift[1]))
    value_pre = split_heads(low_back(matmul(normed_one, qkv_full[2]) + qkv_shift[2]))
    query = low(rotate(query_pre, cos_table, sine_table) * HEAD_DIM ** (-0.5))
    keys = low(rotate(key_pre, cos_table, sine_table))
    values = low(value_pre)
    allowed = allowed_keys(segment_row, 0, SEQ)

    def one_head(operands):
        query_head, key_head, value_head = operands
        scores = low_back(matmul(query_head, key_head.T))
        scores = jnp.where(allowed, scores, -1e+30)
        soft_weights = jax.nn.softmax(scores, axis=-1)
        return matmul(low(soft_weights), value_head)
    attended = lax.map(jax.checkpoint(one_head), (jnp.swapaxes(query, 0, 1), jnp.swapaxes(keys, 0, 1), jnp.swapaxes(values, 0, 1)))
    attended = low(low_back(jnp.swapaxes(attended, 0, 1).reshape(SEQ, D)))
    gate_in = low_back(matmul(normed_two, up_full) + up_shift)
    active = low(jax.nn.gelu(gate_in, approximate=False))
    return seq_rows + matmul(attended, dense_full) + matmul(active, down_full) + out_shift

def reference(hidden_in, first_gain, first_shift, second_gain, second_shift, qkv_weight, qkv_bias, dense_weight, up_weight, up_bias, down_weight, out_bias, segments, positions, cotangent):
    parameters = tuple((item.astype(jnp.float32) for item in (first_gain, first_shift, second_gain, second_shift, qkv_weight, qkv_bias, dense_weight, up_weight, up_bias, down_weight, out_bias)))

    def step(grad_totals, operands):
        seq_rows, segment_row, position_row, seq_cotangent = operands

        def apply_layer(layer_params, layer_rows):
            return one_layer(layer_params, layer_rows, segment_row, position_row)
        layer_out, layer_back = jax.vjp(apply_layer, parameters, seq_rows.astype(jnp.float32))
        grad_params, grad_rows = layer_back(seq_cotangent.astype(jnp.float32))
        grad_totals = jax.tree.map(jnp.add, grad_totals, grad_params)
        return (grad_totals, (layer_out.astype(jnp.bfloat16), grad_rows))
    zero_grads = jax.tree.map(jnp.zeros_like, parameters)
    grad_totals, (outputs, input_grad) = lax.scan(step, zero_grads, (hidden_in, segments, positions, cotangent))
    return (outputs, input_grad, grad_totals[4], grad_totals[5], grad_totals[6], grad_totals[7], grad_totals[8], grad_totals[9], grad_totals[10], grad_totals[0], grad_totals[1], grad_totals[2], grad_totals[3])
```

```python
import jax
import jax.numpy as jnp
from jax import lax
from jax.experimental import pallas as pl
from jax.experimental.pallas import tpu as pltpu
from jax.sharding import PartitionSpec as P

D = 1024
HD = 64
SEQ = 1024
F = 512
C = 128
EPS = 1e-05
f32 = jnp.float32
bf16 = jnp.bfloat16
NSEM = 128

YZ = ("yu", "yw", "zu", "zw")
ORD = tuple(tuple(YZ[(q + s) % 4] for s in range(4)) for q in range(4))

SEM_GH = 0
SEM_GC = 12
SEM_RA = 24
SEM_RD = 34
SEM_F = 44
SEM_W = 76
SEM_S = 108


def dot(a, b):
    return lax.dot_general(a, b, (((1,), (0,)), ((), ())), preferred_element_type=f32)


def dot_nt(a, b):
    return lax.dot_general(a, b, (((1,), (1,)), ((), ())), preferred_element_type=f32)


def dot_tn(a, b):
    return lax.dot_general(a, b, (((0,), (0,)), ((), ())), preferred_element_type=f32)


def kernel_body(
    hid_ref, cot_ref, seg_ref, pos_ref, prm_ref, wqkv_ref, wd_ref, wup_ref, wdn_ref,
    act_out, ing_out, of_out, ow_out, sm_out,
    hidf, cotf, xh, n1, n2, act_s, gel, gg, qs, ks, vs, ga, vT, kT, attT, att, gp,
    dk, dv, wcat, wcatT, wupT, wdnT, wdT, ct, st, segc, po, dxh,
    gf, rf, gw, rw, sa, ra, ssa, r1a, r2a, sd, rd, ssd, r1d, r2d, smv, smr,
    ssem, rsem,
):
    dp = lax.axis_index("dp")
    tn = lax.axis_index("tensor")
    c = tn % 2
    x = tn // 2
    y = dp % 4
    z = dp // 4

    def flip(v):
        return v + 1 - 2 * (v % 2)

    def ub(v):
        return (v + v // 2) % 2

    def wb(v):
        return v // 2

    peer = {
        "c": (dp, x * 2 + 1 - c),
        "xu": (dp, flip(x) * 2 + c),
        "xw": (dp, (3 - x) * 2 + c),
        "yu": (z * 4 + flip(y), tn),
        "yw": (z * 4 + 3 - y, tn),
        "zu": (flip(z) * 4 + y, tn),
        "zw": ((3 - z) * 4 + y, tn),
    }
    bit = {"yu": ub(y), "yw": wb(y), "zu": ub(z), "zw": wb(z)}
    xu, xw = ub(x), wb(x)

    pending = []

    def send(i, src, dst, who):
        cp = pltpu.make_async_remote_copy(
            src_ref=src, dst_ref=dst, send_sem=ssem.at[i], recv_sem=rsem.at[i],
            device_id=peer[who], device_id_type=pl.DeviceIdType.MESH,
        )
        cp.start()
        pending.append(cp)
        return cp

    barrier = pltpu.get_barrier_semaphore()
    for who in peer:
        pl.semaphore_signal(barrier, inc=1, device_id=peer[who], device_id_type=pl.DeviceIdType.MESH)
    pl.semaphore_wait(barrier, len(peer))

    own = pl.multiple_of(tn * 128, 128)
    tu = pl.multiple_of((flip(x) * 2 + c) * 128, 128)
    tw = pl.multiple_of(((3 - x) * 2 + c) * 128, 128)
    x2 = flip(3 - x)
    tuw = pl.multiple_of((x2 * 2 + c) * 128, 128)

    class Gather:
        def __init__(self, src, full, base):
            self.src, self.full, self.b, self.cp = src, full, base, {}

        def go(self, i, src, dst, who):
            self.cp[i] = send(self.b + i, src, dst, who)

        def fwd(self, i, row, n, who):
            ref = self.full.at[pl.ds(row, n)]
            self.go(i, ref, ref, who)

        def start(self):
            lo, hi = self.src.at[0, pl.ds(0, 64)], self.src.at[0, pl.ds(64, 64)]
            dlo, dhi = self.full.at[pl.ds(own, 64)], self.full.at[pl.ds(own + 64, 64)]
            self.go(1, lo, dlo, "xu")
            self.go(2, hi, dhi, "xw")
            self.go(3, hi, dhi, "xu")
            self.go(4, lo, dlo, "xw")
            self.go(0, self.src.at[0], self.full.at[pl.ds(own, 128)], "c")
            self.full[pl.ds(own, 128), :] = self.src[0]

        def mid(self):
            self.cp[1].wait_recv()
            self.fwd(5, tu, 64, "xw")
            self.cp[2].wait_recv()
            self.fwd(6, tw + 64, 64, "xu")

        def d2d(self):
            self.cp[3].wait_recv()
            self.fwd(7, tu, 128, "c")
            self.cp[4].wait_recv()
            self.fwd(8, tw, 128, "c")

        def last(self):
            self.cp[5].wait_recv()
            self.cp[6].wait_recv()
            self.fwd(9, tuw, 128, "c")

        def finish(self):
            for i in (0, 7, 8, 9):
                self.cp[i].wait_recv()

    gh = Gather(hid_ref, hidf, SEM_GH)
    gc = Gather(cot_ref, cotf, SEM_GC)
    gh.start()

    lane = lax.broadcasted_iota(jnp.int32, (1, C), 1)
    for i in range(3):
        wcat[:, i * C:(i + 1) * C] = wqkv_ref[i]
        wcatT[i * C:(i + 1) * C, :] = wqkv_ref[i].T
    wdT[...] = wd_ref[...].T

    @pl.loop(0, 4)
    def _(i):
        r = pl.ds(pl.multiple_of(i * 128, 128), 128)
        wdnT[:, r] = wdn_ref[r, :].T
        wupT[r, :] = wup_ref[:, r].T

    freq = prm_ref[6:7, 0:C]
    sign = prm_ref[6:7, C:2 * C]

    @pl.loop(0, 8)
    def _(i):
        r = pl.ds(pl.multiple_of(i * 128, 128), 128)
        pcol = jnp.broadcast_to(pos_ref[0:1, r].astype(f32), (128, 128)).T
        phase = pcol * freq
        ct[r, :] = jnp.cos(phase)
        st[r, :] = jnp.sin(phase) * sign
        segc[r, :] = jnp.broadcast_to(seg_ref[0:1, r].astype(f32), (128, 128)).T

    gh.mid()
    gc.start()
    gh.d2d()
    gh.last()
    gh.finish()

    g1 = prm_ref[0:1, :]
    b1 = prm_ref[1:2, :]
    g2 = prm_ref[2:3, :]
    b2 = prm_ref[3:4, :]
    low8 = (lane % HD) < 8

    def partner(v):
        return jnp.where(low8, pltpu.roll(v, 120, 1), pltpu.roll(v, 8, 1))

    def norm_stats(xb):
        mu = jnp.mean(xb, axis=1, keepdims=True)
        xc = xb - mu
        rstd = lax.rsqrt(jnp.mean(xc * xc, axis=1, keepdims=True) + EPS)
        return xc * rstd, rstd

    def forward_rows(i):
        r = pl.ds(pl.multiple_of(i * 256, 256), 256)
        xhat, _ = norm_stats(hidf[r, :].astype(f32))
        xh[r, :] = xhat.astype(bf16)
        m1 = (xhat * g1 + b1).astype(bf16)
        m2 = (xhat * g2 + b2).astype(bf16)
        n1[r, :] = m1
        n2[r, :] = m2
        gate = dot(m2, wup_ref[...]) + prm_ref[5:6, 0:F]
        cdf = 0.5 * (1.0 + lax.erf(gate * 0.7071067811865476))
        act_s[r, :] = (gate * cdf).astype(bf16)
        gel[r, :] = cdf + gate * (jnp.exp(-0.5 * gate * gate) * 0.3989422804014327)
        pr = dot(m1, wcat[...]) + prm_ref[5:6, F:F + 3 * C]
        cb, sb = ct[r, :], st[r, :]
        qp, kp, vp = pr[:, 0:C], pr[:, C:2 * C], pr[:, 2 * C:]
        qs[r, :] = ((qp * cb + partner(qp) * sb) * 0.125).astype(bf16)
        kr = kp * cb + partner(kp) * sb
        ks[r, :] = kr.astype(bf16)
        vs[r, :] = vp.astype(bf16)
        kT[:, r] = kr.T.astype(bf16)
        vT[:, r] = vp.T.astype(bf16)

    pl.loop(0, 2)(forward_rows)
    gc.mid()
    pl.loop(2, 4)(forward_rows)
    gc.d2d()
    gc.last()
    gc.finish()

    smv[0] = jnp.zeros((8, D), f32)
    smv[0, 0:1, :] = jnp.sum(cot_ref[0].astype(f32), axis=0, keepdims=True)

    @pl.loop(0, 4)
    def _(i):
        r = pl.ds(pl.multiple_of(i * 256, 256), 256)
        cb = cotf[r, :]
        gb = (dot(cb, wdnT[...]) * gel[r, :]).astype(bf16)
        gg[r, :] = gb
        smv[0, 5:6, 0:F] += jnp.sum(gb.astype(f32), axis=0, keepdims=True)
        ga[r, :] = dot(cb, wdT[...]).astype(bf16)

    class AllReduce:
        def __init__(self, g, rr, o, base, n):
            self.g, self.r, self.o, self.b, self.n = g, rr, o, base, n
            self.off = {}
            self.cp = {}

        def rows(self, s):
            return self.n >> (s + 1)

        def start(self, s, qs_=range(4)):
            h = self.rows(s)
            for q in qs_:
                off = self.off[q, s] if s else 0
                b = bit[ORD[q][s]]
                self.off[q, s + 1] = pl.multiple_of(off + b * h, h)
                src = pl.multiple_of(off + (1 - b) * h, h)
                roff = self.n - 2 * h
                self.cp[q, s] = send(
                    self.b + q * 8 + s, self.g.at[q, pl.ds(src, h)], self.r.at[q, pl.ds(roff, h)], ORD[q][s]
                )

        def add(self, s, qs_=range(4)):
            h = self.rows(s)
            roff = self.n - 2 * h
            for q in qs_:
                self.cp[q, s].wait_recv()
                keep = pl.ds(self.off[q, s + 1], h)
                tot = self.g[q, keep, :].astype(f32) + self.r[q, pl.ds(roff, h), :].astype(f32)
                if s == 3:
                    self.o[q, keep, :] = tot.astype(bf16)
                else:
                    self.g[q, keep, :] = tot.astype(bf16)

        def step(self, s):
            self.add(s)
            if s < 3:
                self.start(s + 1)
            else:
                self.spread(3)

        def spread(self, s):
            h = self.rows(s)
            for q in range(4):
                ref = self.o.at[q, pl.ds(self.off[q, s + 1], h)]
                self.cp[q, 7 - s] = send(self.b + q * 8 + 7 - s, ref, ref, ORD[q][s])

        def back(self, s):
            for q in range(4):
                self.cp[q, 7 - s].wait_recv()
            if s > 0:
                self.spread(s - 1)

    arf = AllReduce(gf, rf, of_out, SEM_F, 256)
    arw = AllReduce(gw, rw, ow_out, SEM_W, 1024)

    for j in range(2):
        @pl.loop(0, 2)
        def _(i, j=j):
            cc = pl.ds(pl.multiple_of(i * 512, 512), 512)
            gf[j, :, cc] = dot_tn(act_s[:, j * 256:(j + 1) * 256], cotf[:, cc]).astype(bf16)

        arf.start(0, (j,))
    for j in range(2):
        @pl.loop(0, 2)
        def _(i, j=j):
            rr = pl.ds(pl.multiple_of(j * 512 + i * 256, 256), 256)
            cc = pl.ds(pl.multiple_of(i * 512, 512), 512)
            gf[2 + j, :, cc] = dot_tn(n2[:, rr], gg[...]).astype(bf16)

        arf.start(0, (2 + j,))

    @pl.loop(0, 4)
    def _(i):
        r = pl.ds(pl.multiple_of(i * 256, 256), 256)
        po[r, :] = dot(act_s[r, :], wdn_ref[...])
        g2c = dot(gg[r, :], wupT[...])
        smv[0, 3:4, :] += jnp.sum(g2c * xh[r, :].astype(f32), axis=0, keepdims=True)
        smv[0, 4:5, :] += jnp.sum(g2c, axis=0, keepdims=True)
        dxh[r, :] = g2c * g2

    arf.step(0)

    dk[...] = jnp.zeros_like(dk)
    dv[...] = jnp.zeros_like(dv)

    def attention_block(i):
        q0, L = i * 256, (i + 1) * 256
        qb, gb = qs[q0:L, :], ga[q0:L, :]
        zero = jnp.zeros((), bf16)
        kidx = lax.broadcasted_iota(jnp.int32, (L, 256), 0)
        qidx = lax.broadcasted_iota(jnp.int32, (L, 256), 1) + q0
        sc = segc[0:L, :]
        same = jnp.concatenate([sc, sc], axis=1) == seg_ref[0:1, q0:L].astype(f32)
        allowed = same & (kidx <= qidx)
        pbs, dss, qms, gms, outs, dqs = [], [], [], [], [], []
        for h in range(2):
            mine = (lane // HD) == h
            qm, gm = jnp.where(mine, qb, zero), jnp.where(mine, gb, zero)
            s = jnp.where(allowed, dot_nt(ks[0:L, :], qm), -1e30)
            e = jnp.exp(s - jnp.max(s, axis=0, keepdims=True))
            p = e / jnp.sum(e, axis=0, keepdims=True)
            pb = p.astype(bf16)
            dp_ = dot_nt(vs[0:L, :], gm)
            ds = (p * (dp_ - jnp.sum(p * dp_, axis=0, keepdims=True))).astype(bf16)
            outs.append(dot(vT[h * HD:(h + 1) * HD, 0:L], pb))
            dqs.append(dot(kT[h * HD:(h + 1) * HD, 0:L], ds))
            pbs.append(pb)
            dss.append(ds)
            qms.append(qm)
            gms.append(gm)
        dv[0:L, :] += dot(jnp.concatenate(pbs, axis=1), jnp.concatenate(gms, axis=0))
        dk[0:L, :] += dot(jnp.concatenate(dss, axis=1), jnp.concatenate(qms, axis=0))
        oT = jnp.concatenate(outs, axis=0)
        attT[:, q0:L] = oT.astype(bf16)
        att[q0:L, :] = oT.T.astype(bf16)
        dq = jnp.concatenate(dqs, axis=0).T
        dq = (dq * ct[q0:L, :] - partner(dq) * st[q0:L, :]) * 0.125
        gp[q0:L, 0:C] = dq.astype(bf16)

    attention_block(0)
    attention_block(1)
    arf.step(1)
    attention_block(2)
    arf.step(2)
    attention_block(3)
    arf.step(3)

    @pl.loop(0, 4)
    def _(i):
        r = pl.ds(pl.multiple_of(i * 256, 256), 256)
        dkb = dk[r, :]
        gp[r, C:2 * C] = (dkb * ct[r, :] - partner(dkb) * st[r, :]).astype(bf16)
        gp[r, 2 * C:] = dv[r, :].astype(bf16)
        smv[0, 5:6, F:F + 3 * C] += jnp.sum(gp[r, :].astype(f32), axis=0, keepdims=True)

    arf.back(3)

    @pl.loop(0, 4)
    def _(i):
        r = pl.ds(pl.multiple_of(i * 256, 256), 256)
        res = dot_tn(n1[:, r], gp[...]).astype(bf16)
        gw[0, r, :] = res[:, 0:C]
        gw[1, r, :] = res[:, C:2 * C]
        gw[2, r, :] = res[:, 2 * C:]
        dn = dot(attT[...], cotf[:, r]).astype(bf16)
        gw[3, pl.ds(pl.multiple_of(i * 256, 256), 128), :] = dn[:, 0:C]
        gw[3, pl.ds(pl.multiple_of(i * 256 + 128, 128), 128), :] = dn[:, C:]

    arw.start(0)
    arf.back(2)

    class Scatter:
        def __init__(self, full, s0, r0, ss, r1, r2, base):
            self.full, self.s0, self.r0, self.ss, self.r1, self.r2, self.b = full, s0, r0, ss, r1, r2, base
            self.cp = {}

        def give(self):
            for i in range(4):
                row = pl.multiple_of(i * 256 + (1 - c) * 128, 128)
                self.s0[i] = self.full[pl.ds(row, 128), :].astype(bf16)
                self.cp[i] = send(self.b + i, self.s0.at[i], self.r0.at[i], "c")

        def fold(self):
            for u in range(2):
                for w in range(2):
                    i = 2 * w + (u ^ w)
                    self.cp[i].wait_recv()
                    row = pl.multiple_of(i * 256 + c * 128, 128)
                    val = (self.full[pl.ds(row, 128), :] + self.r0[i].astype(f32)).astype(bf16)
                    self.ss[0, u, w] = val[0:64]
                    self.ss[1, w, u] = val[64:128]
            self.cp[4] = send(self.b + 4, self.ss.at[0, 1 - xu], self.r1.at[0], "xu")
            self.cp[5] = send(self.b + 5, self.ss.at[1, 1 - xw], self.r1.at[1], "xw")

        def second(self):
            self.cp[4].wait_recv()
            for w in range(2):
                self.r1[0, w] = (self.r1[0, w].astype(f32) + self.ss[0, xu, w].astype(f32)).astype(bf16)
            self.cp[6] = send(self.b + 6, self.r1.at[0, 1 - xw], self.r2.at[0], "xw")
            self.cp[5].wait_recv()
            for u in range(2):
                self.r1[1, u] = (self.r1[1, u].astype(f32) + self.ss[1, xw, u].astype(f32)).astype(bf16)
            self.cp[7] = send(self.b + 7, self.r1.at[1, 1 - xu], self.r2.at[1], "xu")

        def result(self, half):
            self.cp[6 + half].wait_recv()
            mine = self.r1[0, xw] if half == 0 else self.r1[1, xu]
            return mine.astype(f32) + self.r2[half].astype(f32)

    rsa = Scatter(po, sa, ra, ssa, r1a, r2a, SEM_RA)
    rsd = Scatter(dxh, sd, rd, ssd, r1d, r2d, SEM_RD)

    @pl.loop(0, 4)
    def _(i):
        r = pl.ds(pl.multiple_of(i * 256, 256), 256)
        g1c = dot(gp[r, :], wcatT[...])
        smv[0, 1:2, :] += jnp.sum(g1c * xh[r, :].astype(f32), axis=0, keepdims=True)
        smv[0, 2:3, :] += jnp.sum(g1c, axis=0, keepdims=True)
        dxh[r, :] += g1c * g1
        po[r, :] += dot(att[r, :], wd_ref[...])

    DIMS = YZ + ("xu", "xw", "c")
    smc = {}

    def small_start(k):
        smc[k] = send(SEM_S + k, smv.at[k], smr.at[k], DIMS[k])

    def small_step(k):
        smc[k].wait_recv()
        smv[k + 1] = smv[k] + smr[k]
        if k < 6:
            small_start(k + 1)

    small_start(0)
    rsa.give()
    rsd.give()
    arf.back(1)
    rsa.fold()
    rsd.fold()
    arw.step(0)
    small_step(0)
    rsa.second()
    arw.step(1)
    small_step(1)
    rsd.second()
    arw.step(2)
    small_step(2)

    for half in range(2):
        hr = pl.ds(half * 64, 64)
        act = hid_ref[0, hr, :].astype(f32) + rsa.result(half) + prm_ref[4:5, :]
        act_out[hr, :] = act.astype(bf16)
    arw.step(3)
    small_step(3)
    for half in range(2):
        hr = pl.ds(half * 64, 64)
        d = rsd.result(half)
        xhat, rstd = norm_stats(hid_ref[0, hr, :].astype(f32))
        back = (d - jnp.mean(d, axis=1, keepdims=True) - xhat * jnp.mean(d * xhat, axis=1, keepdims=True)) * rstd
        ing_out[hr, :] = cot_ref[0, hr, :].astype(f32) + back
    arw.back(3)
    small_step(4)
    arw.back(2)
    small_step(5)
    arw.back(1)
    small_step(6)
    arf.back(0)
    arw.back(0)
    sm_out[...] = smv[7]
    sm_out[5:6, :] = smv[4, 5:6, :]
    for cp in pending:
        cp.wait_send()


def layer(hid, cot, seg, pos, prm, wqkv, wd, wup, wdn):
    v = lambda s, d: pltpu.VMEM(s, d)
    big = (1024, 1024)
    scratch = [
        v(big, bf16), v(big, bf16), v(big, bf16), v(big, bf16), v(big, bf16),
        v((1024, F), bf16), v((1024, F), f32), v((1024, F), bf16),
        v((1024, C), bf16), v((1024, C), bf16), v((1024, C), bf16), v((1024, C), bf16),
        v((C, 1024), bf16), v((C, 1024), bf16), v((C, 1024), bf16), v((1024, C), bf16),
        v((1024, 3 * C), bf16),
        v((1024, C), f32), v((1024, C), f32),
        v((1024, 3 * C), bf16), v((3 * C, 1024), bf16), v((F, 1024), bf16), v((1024, F), bf16), v((1024, C), bf16),
        v((1024, C), f32), v((1024, C), f32), v((1024, C), f32),
        v(big, f32), v(big, f32),
        v((4, 256, 1024), bf16), v((4, 256, 1024), bf16), v((4, 1024, C), bf16), v((4, 1024, C), bf16),
    ]
    for _ in range(2):
        scratch += [
            v((4, 128, D), bf16), v((4, 128, D), bf16), v((2, 2, 2, 64, D), bf16), v((2, 2, 64, D), bf16),
            v((2, 64, D), bf16),
        ]
    scratch += [v((8, 8, D), f32), v((7, 8, D), f32)]
    scratch += [pltpu.SemaphoreType.DMA((NSEM,)), pltpu.SemaphoreType.DMA((NSEM,))]
    vm = pl.BlockSpec(memory_space=pltpu.VMEM)
    return pl.pallas_call(
        kernel_body,
        out_shape=[
            jax.ShapeDtypeStruct((128, D), bf16),
            jax.ShapeDtypeStruct((128, D), f32),
            jax.ShapeDtypeStruct((4, 256, 1024), bf16),
            jax.ShapeDtypeStruct((4, 1024, C), bf16),
            jax.ShapeDtypeStruct((8, D), f32),
        ],
        in_specs=[vm] * 9,
        out_specs=[vm] * 5,
        scratch_shapes=scratch,
        compiler_params=pltpu.CompilerParams(
            collective_id=0, has_side_effects=True, vmem_limit_bytes=63 * 1024 * 1024
        ),
    )(hid, cot, seg, pos, prm, wqkv, wd, wup, wdn)


def local(
    hidden_in, first_gain, first_shift, second_gain, second_shift, qkv_weight, qkv_bias, dense_weight,
    up_weight, up_bias, down_weight, out_bias, segments, positions, cotangent,
):
    freq = 10000.0 ** (-2.0 * jnp.arange(8, dtype=f32) / 16)
    zeros = jnp.zeros((48,), f32)
    head_freq = jnp.concatenate([freq, freq, zeros])
    head_sign = jnp.concatenate([-jnp.ones((8,), f32), jnp.ones((8,), f32), zeros])
    consts = jnp.concatenate([head_freq, head_freq, head_sign, head_sign, jnp.zeros((768,), f32)])
    biases = jnp.concatenate([up_bias, qkv_bias.reshape(3 * C), jnp.zeros((128,), bf16)]).astype(f32)
    rows = [first_gain, first_shift, second_gain, second_shift, out_bias]
    prm = jnp.stack([r.astype(f32) for r in rows] + [biases, consts, jnp.zeros((D,), f32)])
    act, ing, of, ow, sm = layer(
        hidden_in, cotangent, segments, positions, prm, qkv_weight, dense_weight, up_weight, down_weight
    )
    grad_down = of[0:2].reshape(F, D).astype(f32)
    grad_up = of[2:4].reshape(2, 256, 2, F).transpose(0, 2, 1, 3).reshape(D, F).astype(f32)
    grad_qkv = ow[0:3].astype(f32)
    grad_dense = ow[3].reshape(8, C, C).transpose(1, 0, 2).reshape(C, D).astype(f32)
    return (
        act[None], ing[None], grad_qkv, sm[5, F:F + 3 * C].reshape(3, C), grad_dense, grad_up, sm[5, 0:F],
        grad_down, sm[0], sm[1], sm[2], sm[3], sm[4],
    )


def solution(mesh):
    placed = (
        P("dp", "tensor", None), P(), P(), P(), P(), P(None, None, "tensor"), P(None, "tensor"),
        P("tensor", None), P(None, "tensor"), P("tensor"), P("tensor", None), P(), P("dp", None),
        P("dp", None), P("dp", "tensor", None),
    )
    return jax.shard_map(
        local,
        mesh=mesh,
        in_specs=placed,
        out_specs=(
            P("dp", "tensor", None), P("dp", "tensor", None), P(None, None, "tensor"), P(None, "tensor"),
            P("tensor", None), P(None, "tensor"), P("tensor"), P("tensor", None), P(), P(), P(), P(), P(),
        ),
        check_vma=False,
    )
```

```python
import jax
import jax.numpy as jnp
from jax import lax
from jax.experimental import pallas as pl
from jax.experimental.pallas import tpu as pltpu
from jax.sharding import PartitionSpec as P

D = 1024
HD = 64
SEQ = 1024
F = 512
C = 128
EPS = 1e-05
f32 = jnp.float32
bf16 = jnp.bfloat16
NSEM = 176

YZ = ("yu", "yw", "zu", "zw")
ORD = tuple(tuple(YZ[(q + s) % 4] for s in range(4)) for q in range(4))


def dot(a, b):
    return lax.dot_general(a, b, (((1,), (0,)), ((), ())), preferred_element_type=f32)


def dot_nt(a, b):
    return lax.dot_general(a, b, (((1,), (1,)), ((), ())), preferred_element_type=f32)


def dot_tn(a, b):
    return lax.dot_general(a, b, (((0,), (0,)), ((), ())), preferred_element_type=f32)


def column(row, n):
    return jnp.broadcast_to(row.astype(f32), (n, row.shape[1])).T


def kernel_body(
    hid_ref, cot_ref, seg_ref, pos_ref, g1_ref, b1_ref, g2_ref, b2_ref, ob_ref, ub_ref, qb_ref,
    wqkv_ref, wd_ref, wup_ref, wdn_ref,
    act_out, ing_out, od_out, ou_out, ow_out, sm_out,
    hidf, cotf, xh, n1, n2, act_s, gel, gg, qs, ks, vs, ga, vT, kT, attT, att, gp,
    dk, dv, wqkv, wd, wup, wdn, wcat, wcatT, wupT, wdnT, wdT, ct, st, segc, po, dxh,
    gd, rd_, od, gu, ru_, ou, gw, rw1, pw, rw2, ow,
    sa, ra, ssa, r1a, r2a, sd, rd, ssd, r1d, r2d, sm, smy, smz, smt,
    ssem, rsem, lsem,
):
    dp = lax.axis_index("dp")
    tn = lax.axis_index("tensor")
    c = tn % 2
    x = tn // 2
    y = dp % 4
    z = dp // 4

    def flip(v):
        return v + 1 - 2 * (v % 2)

    def ub(v):
        return (v + v // 2) % 2

    def wb(v):
        return v // 2

    peer = {
        "c": (dp, x * 2 + 1 - c),
        "xu": (dp, flip(x) * 2 + c),
        "xw": (dp, (3 - x) * 2 + c),
        "yu": (z * 4 + flip(y), tn),
        "yw": (z * 4 + 3 - y, tn),
        "zu": (flip(z) * 4 + y, tn),
        "zw": ((3 - z) * 4 + y, tn),
    }
    ring = []
    for k in range(1, 4):
        peer["y", k] = (z * 4 + (y + k) % 4, tn)
        peer["z", k] = (((z + k) % 4) * 4 + y, tn)
        ring += [("y", k), ("z", k)]
    for k in range(1, 8):
        peer["t", k] = (dp, (tn + k) % 8)
        ring.append(("t", k))
    bit = {"yu": ub(y), "yw": wb(y), "zu": ub(z), "zw": wb(z)}
    xu, xw = ub(x), wb(x)

    pending = []
    count = [0]

    def send(src, dst, who):
        i = count[0]
        count[0] += 1
        cp = pltpu.make_async_remote_copy(
            src_ref=src, dst_ref=dst, send_sem=ssem.at[i], recv_sem=rsem.at[i],
            device_id=peer[who], device_id_type=pl.DeviceIdType.MESH,
        )
        cp.start()
        pending.append(cp)
        return cp

    own = pl.multiple_of(tn * 128, 128)
    own_rows = pl.ds(own, 128)
    moves = []

    def move(src, dst):
        cp = pltpu.make_async_copy(src, dst, lsem.at[len(moves)])
        cp.start()
        moves.append(cp)
        return cp

    m_hid = move(hid_ref.at[0], hidf.at[own_rows])
    m_cot = move(cot_ref.at[0], cotf.at[own_rows])
    m_w = [move(wqkv_ref, wqkv), move(wd_ref, wd), move(wup_ref, wup), move(wdn_ref, wdn)]

    barrier = pltpu.get_barrier_semaphore()
    for who in ring:
        pl.semaphore_signal(barrier, inc=1, device_id=peer[who], device_id_type=pl.DeviceIdType.MESH)
    pl.semaphore_wait(barrier, len(ring))

    x2 = flip(3 - x)
    tu = pl.multiple_of((flip(x) * 2 + c) * 128, 128)
    tw = pl.multiple_of(((3 - x) * 2 + c) * 128, 128)
    tuw = pl.multiple_of((x2 * 2 + c) * 128, 128)
    row_own = pl.multiple_of(x * 256, 256)
    row_u = pl.multiple_of(flip(x) * 256, 256)
    row_w = pl.multiple_of((3 - x) * 256, 256)
    row_uw = pl.multiple_of(x2 * 256, 256)

    class Gather:
        def __init__(self, src, full):
            self.src, self.full, self.cp = src, full, {}

        def fwd(self, i, row, n, who):
            ref = self.full.at[pl.ds(row, n)]
            self.cp[i] = send(ref, ref, who)

        def start_core(self):
            self.cp[0] = send(self.src.at[0], self.full.at[own_rows], "c")

        def start(self):
            lo, hi = self.src.at[0, pl.ds(0, 64)], self.src.at[0, pl.ds(64, 64)]
            dlo, dhi = self.full.at[pl.ds(own, 64)], self.full.at[pl.ds(own + 64, 64)]
            self.cp[1] = send(lo, dlo, "xu")
            self.cp[2] = send(hi, dhi, "xw")
            self.cp[3] = send(hi, dhi, "xu")
            self.cp[4] = send(lo, dlo, "xw")

        def mid(self):
            self.cp[1].wait_recv()
            self.fwd(5, tu, 64, "xw")
            self.cp[2].wait_recv()
            self.fwd(6, tw + 64, 64, "xu")

        def d2d(self):
            self.cp[3].wait_recv()
            self.fwd(7, tu, 128, "c")
            self.cp[4].wait_recv()
            self.fwd(8, tw, 128, "c")

        def last(self):
            self.cp[5].wait_recv()
            self.cp[6].wait_recv()
            self.fwd(9, tuw, 128, "c")

        def ready(self, i):
            self.cp[i].wait_recv()

    gh = Gather(hid_ref, hidf)
    gc = Gather(cot_ref, cotf)
    gh.start()
    gh.start_core()

    lane = lax.broadcasted_iota(jnp.int32, (1, C), 1)
    turn = lane % 8
    freq = jnp.zeros((1, C), f32)
    for j in range(8):
        freq = jnp.where(turn == j, 10000.0 ** (-2.0 * j / 16), freq)
    place = lane % HD
    freq = jnp.where(place < 16, freq, 0.0)
    sign = jnp.where(place < 8, -1.0, 1.0)
    low8 = place < 8

    @pl.loop(0, 8)
    def _(i):
        r = pl.ds(pl.multiple_of(i * 128, 128), 128)
        phase = column(pos_ref[0:1, r], 128) * freq
        ct[r, :] = jnp.cos(phase)
        st[r, :] = jnp.sin(phase) * sign
        segc[r, :] = column(seg_ref[0:1, r], 128)

    for cp in m_w:
        cp.wait()
    m_hid.wait()
    m_cot.wait()
    for i in range(3):
        wcat[:, i * C:(i + 1) * C] = wqkv[i]
        wcatT[i * C:(i + 1) * C, :] = wqkv[i].T

    gh.mid()
    gc.start()
    gc.start_core()

    wdT[...] = wd[...].T

    @pl.loop(0, 4)
    def _(i):
        r = pl.ds(pl.multiple_of(i * 128, 128), 128)
        wdnT[:, r] = wdn[r, :].T
        wupT[r, :] = wup[:, r].T

    def row_of(ref):
        return ref[...].astype(f32).reshape(1, -1)

    g1, b1, g2, b2 = row_of(g1_ref), row_of(b1_ref), row_of(g2_ref), row_of(b2_ref)
    up_b = row_of(ub_ref)
    qb_all = qb_ref[...].astype(f32)
    qkv_b = jnp.concatenate([qb_all[i:i + 1] for i in range(3)], axis=1)

    def partner(v):
        return jnp.where(low8, pltpu.roll(v, 120, 1), pltpu.roll(v, 8, 1))

    def norm_stats(xb):
        mu = jnp.mean(xb, axis=1, keepdims=True)
        xc = xb - mu
        rstd = lax.rsqrt(jnp.mean(xc * xc, axis=1, keepdims=True) + EPS)
        return xc * rstd, rstd

    def forward_rows(base):
        r = pl.ds(base, 256)
        xhat, _ = norm_stats(hidf[r, :].astype(f32))
        xh[r, :] = xhat.astype(bf16)
        m1 = (xhat * g1 + b1).astype(bf16)
        m2 = (xhat * g2 + b2).astype(bf16)
        n1[r, :] = m1
        n2[r, :] = m2
        gate = dot(m2, wup[...]) + up_b
        cdf = 0.5 * (1.0 + lax.erf(gate * 0.7071067811865476))
        act_s[r, :] = (gate * cdf).astype(bf16)
        gel[r, :] = cdf + gate * (jnp.exp(-0.5 * gate * gate) * 0.3989422804014327)
        pr = dot(m1, wcat[...]) + qkv_b
        cb, sb = ct[r, :], st[r, :]
        qp, kp, vp = pr[:, 0:C], pr[:, C:2 * C], pr[:, 2 * C:]
        qs[r, :] = ((qp * cb + partner(qp) * sb) * 0.125).astype(bf16)
        kr = kp * cb + partner(kp) * sb
        ks[r, :] = kr.astype(bf16)
        vs[r, :] = vp.astype(bf16)
        kT[:, r] = kr.T.astype(bf16)
        vT[:, r] = vp.T.astype(bf16)

    def backward_rows(base):
        r = pl.ds(base, 256)
        cb = cotf[r, :]
        gb = (dot(cb, wdnT[...]) * gel[r, :]).astype(bf16)
        gg[r, :] = gb
        sm[5:6, 0:F] += jnp.sum(gb.astype(f32), axis=0, keepdims=True)
        ga[r, :] = dot(cb, wdT[...]).astype(bf16)

    sm[...] = jnp.zeros((8, D), f32)
    sm[0:1, :] = jnp.sum(cotf[own_rows, :].astype(f32), axis=0, keepdims=True)

    gh.ready(0)
    forward_rows(row_own)
    gh.d2d()
    gh.ready(7)
    forward_rows(row_u)
    gh.last()
    gh.ready(8)
    forward_rows(row_w)
    gc.mid()
    gh.ready(9)
    forward_rows(row_uw)
    gc.d2d()
    gc.ready(0)
    backward_rows(row_own)
    gc.last()
    gc.ready(7)
    backward_rows(row_u)
    gc.ready(8)
    backward_rows(row_w)
    gc.ready(9)

    class AllReduce:
        def __init__(self, g, rr, o, n):
            self.g, self.r, self.o, self.n = g, rr, o, n
            self.off = {}
            self.cp = {}

        def rows(self, s):
            return self.n >> (s + 1)

        def start(self, s, qs_=range(4)):
            h = self.rows(s)
            for q in qs_:
                off = self.off[q, s] if s else 0
                b = bit[ORD[q][s]]
                self.off[q, s + 1] = pl.multiple_of(off + b * h, h)
                src = pl.multiple_of(off + (1 - b) * h, h)
                roff = self.n - 2 * h
                self.cp[q, s] = send(self.g.at[q, pl.ds(src, h)], self.r.at[q, pl.ds(roff, h)], ORD[q][s])

        def step(self, s):
            h = self.rows(s)
            roff = self.n - 2 * h
            for q in range(4):
                self.cp[q, s].wait_recv()
                keep = pl.ds(self.off[q, s + 1], h)
                tot = (self.g[q, keep, :].astype(f32) + self.r[q, pl.ds(roff, h), :].astype(f32)).astype(bf16)
                if s == 3:
                    self.o[q, keep, :] = tot
                    self.spread(3, (q,))
                else:
                    self.g[q, keep, :] = tot
                    self.start(s + 1, (q,))

        def spread(self, s, qs_=range(4)):
            h = self.rows(s)
            for q in qs_:
                ref = self.o.at[q, pl.ds(self.off[q, s + 1], h)]
                self.cp[q, 7 - s] = send(ref, ref, ORD[q][s])

        def back(self, s):
            for q in range(4):
                self.cp[q, 7 - s].wait_recv()
                if s > 0:
                    self.spread(s - 1, (q,))

    ard = AllReduce(gd, rd_, od, 256)
    aru = AllReduce(gu, ru_, ou, 256)

    for q in range(4):
        f0, d0 = 256 * (q // 2), 512 * (q % 2)
        gd[q] = dot_tn(act_s[:, f0:f0 + 256], cotf[:, d0:d0 + 512]).astype(bf16)
        ard.start(0, (q,))
    backward_rows(row_uw)
    for q in range(4):
        gu[q] = dot_tn(n2[:, 256 * q:256 * (q + 1)], gg[...]).astype(bf16)
        aru.start(0, (q,))

    dk[...] = jnp.zeros_like(dk)
    dv[...] = jnp.zeros_like(dv)

    def attention_block(i):
        q0, L = i * 256, (i + 1) * 256
        qb, gb = qs[q0:L, :], ga[q0:L, :]
        zero = jnp.zeros((), bf16)
        kidx = lax.broadcasted_iota(jnp.int32, (L, 256), 0)
        qidx = lax.broadcasted_iota(jnp.int32, (L, 256), 1) + q0
        sc = segc[0:L, :]
        same = jnp.concatenate([sc, sc], axis=1) == seg_ref[0:1, q0:L].astype(f32)
        allowed = same & (kidx <= qidx)
        pbs, dss, qms, gms, outs, dqs = [], [], [], [], [], []
        for h in range(2):
            mine = (lane // HD) == h
            qm, gm = jnp.where(mine, qb, zero), jnp.where(mine, gb, zero)
            s = jnp.where(allowed, dot_nt(ks[0:L, :], qm), -1e30)
            e = jnp.exp(s - jnp.max(s, axis=0, keepdims=True))
            p = e * (1.0 / jnp.sum(e, axis=0, keepdims=True))
            pb = p.astype(bf16)
            dp_ = dot_nt(vs[0:L, :], gm)
            ds = (p * (dp_ - jnp.sum(p * dp_, axis=0, keepdims=True))).astype(bf16)
            outs.append(dot(vT[h * HD:(h + 1) * HD, 0:L], pb))
            dqs.append(dot(kT[h * HD:(h + 1) * HD, 0:L], ds))
            pbs.append(pb)
            dss.append(ds)
            qms.append(qm)
            gms.append(gm)
        dv[0:L, :] += dot(jnp.concatenate(pbs, axis=1), jnp.concatenate(gms, axis=0))
        dk[0:L, :] += dot(jnp.concatenate(dss, axis=1), jnp.concatenate(qms, axis=0))
        oT = jnp.concatenate(outs, axis=0)
        attT[:, q0:L] = oT.astype(bf16)
        att[q0:L, :] = oT.T.astype(bf16)
        cb, sb = ct[q0:L, :], st[q0:L, :]
        dq = jnp.concatenate(dqs, axis=0).T
        gp[q0:L, 0:C] = ((dq * cb - partner(dq) * sb) * 0.125).astype(bf16)
        dkb = dk[q0:L, :]
        gp[q0:L, C:2 * C] = (dkb * cb - partner(dkb) * sb).astype(bf16)
        gp[q0:L, 2 * C:] = dv[q0:L, :].astype(bf16)
        sm[5:6, F:F + 3 * C] += jnp.sum(gp[q0:L, :].astype(f32), axis=0, keepdims=True)

    attention_block(3)
    ard.step(0)
    aru.step(0)
    attention_block(2)
    ard.step(1)
    aru.step(1)
    attention_block(1)
    ard.step(2)
    aru.step(2)
    attention_block(0)

    class RingReduce:
        def __init__(self):
            self.ax = (("y", y, "z", z), ("z", z, "y", y))
            self.cp = {}

        def start(self, a):
            ax, me, _, _ = self.ax[a]
            for k in (2, 1, 3):
                to = pl.multiple_of((me + k) % 4 * 256, 256)
                self.cp[a, 0, k] = send(gw.at[pl.ds(2 * a, 2), pl.ds(to, 256)], rw1.at[a, k - 1], (ax, k))

        def step1(self, a):
            _, me, ax, other = self.ax[a]
            for k in (1, 3, 2):
                self.cp[a, 0, k].wait_recv()
            tot = gw[pl.ds(2 * a, 2), pl.ds(pl.multiple_of(me * 256, 256), 256), :].astype(f32)
            for k in range(3):
                tot = tot + rw1[a, k].astype(f32)
            pw[a] = tot.astype(bf16)
            for k in (2, 1, 3):
                to = pl.multiple_of((other + k) % 4 * 64, 64)
                self.cp[a, 1, k] = send(pw.at[a, :, pl.ds(to, 64)], rw2.at[a, k - 1], (ax, k))

        def step2(self, a):
            _, me, ax, other = self.ax[a]
            for k in (1, 3, 2):
                self.cp[a, 1, k].wait_recv()
            tot = pw[a, :, pl.ds(pl.multiple_of(other * 64, 64), 64), :].astype(f32)
            for k in range(3):
                tot = tot + rw2[a, k].astype(f32)
            mine = pl.ds(pl.multiple_of(me * 256 + other * 64, 64), 64)
            ow[pl.ds(2 * a, 2), mine, :] = tot.astype(bf16)
            ref = ow.at[pl.ds(2 * a, 2), mine]
            for k in (2, 1, 3):
                self.cp[a, 2, k] = send(ref, ref, (ax, k))

        def step3(self, a):
            ax, me, _, _ = self.ax[a]
            for k in (1, 3, 2):
                self.cp[a, 2, k].wait_recv()
            ref = ow.at[pl.ds(2 * a, 2), pl.ds(pl.multiple_of(me * 256, 256), 256)]
            for k in (2, 1, 3):
                self.cp[a, 3, k] = send(ref, ref, (ax, k))

        def finish(self, a):
            for k in (1, 3, 2):
                self.cp[a, 3, k].wait_recv()

    arw = RingReduce()

    @pl.loop(0, 4)
    def _(i):
        r = pl.ds(pl.multiple_of(i * 256, 256), 256)
        res = dot_tn(n1[:, r], gp[...]).astype(bf16)
        gw[0, r, :] = res[:, 0:C]
        gw[1, r, :] = res[:, C:2 * C]
        gw[2, r, :] = res[:, 2 * C:]
        dn = dot(attT[...], cotf[:, r]).astype(bf16)
        gw[3, pl.ds(pl.multiple_of(i * 256, 256), 128), :] = dn[:, 0:C]
        gw[3, pl.ds(pl.multiple_of(i * 256 + 128, 128), 128), :] = dn[:, C:]

    arw.start(0)
    arw.start(1)
    ard.step(3)
    aru.step(3)

    class Scatter:
        def __init__(self, full, s0, r0, ss, r1, r2):
            self.full, self.s0, self.r0, self.ss, self.r1, self.r2 = full, s0, r0, ss, r1, r2
            self.cp = {}

        def give(self, i):
            row = pl.multiple_of(i * 256 + (1 - c) * 128, 128)
            self.s0[i] = self.full[pl.ds(row, 128), :].astype(bf16)
            self.cp[i] = send(self.s0.at[i], self.r0.at[i], "c")

        def fold(self):
            for u in range(2):
                for w in range(2):
                    i = 2 * w + (u ^ w)
                    self.cp[i].wait_recv()
                    row = pl.multiple_of(i * 256 + c * 128, 128)
                    val = (self.full[pl.ds(row, 128), :] + self.r0[i].astype(f32)).astype(bf16)
                    self.ss[0, u, w] = val[0:64]
                    self.ss[1, w, u] = val[64:128]
            self.cp[4] = send(self.ss.at[0, 1 - xu], self.r1.at[0], "xu")
            self.cp[5] = send(self.ss.at[1, 1 - xw], self.r1.at[1], "xw")

        def second(self):
            self.cp[4].wait_recv()
            for w in range(2):
                self.r1[0, w] = (self.r1[0, w].astype(f32) + self.ss[0, xu, w].astype(f32)).astype(bf16)
            self.cp[6] = send(self.r1.at[0, 1 - xw], self.r2.at[0], "xw")
            self.cp[5].wait_recv()
            for u in range(2):
                self.r1[1, u] = (self.r1[1, u].astype(f32) + self.ss[1, xw, u].astype(f32)).astype(bf16)
            self.cp[7] = send(self.r1.at[1, 1 - xu], self.r2.at[1], "xu")

        def result(self, half):
            self.cp[6 + half].wait_recv()
            mine = self.r1[0, xw] if half == 0 else self.r1[1, xu]
            return mine.astype(f32) + self.r2[half].astype(f32)

    rsa = Scatter(po, sa, ra, ssa, r1a, r2a)
    rsd = Scatter(dxh, sd, rd, ssd, r1d, r2d)

    for i in range(4):
        r = pl.ds(i * 256, 256)
        po[r, :] = dot(act_s[r, :], wdn[...]) + dot(att[r, :], wd[...])
        rsa.give(i)
    ard.back(3)
    aru.back(3)
    for i in range(4):
        r = pl.ds(i * 256, 256)
        xhb = xh[r, :].astype(f32)
        g1c = dot(gp[r, :], wcatT[...])
        sm[1:2, :] += jnp.sum(g1c * xhb, axis=0, keepdims=True)
        sm[2:3, :] += jnp.sum(g1c, axis=0, keepdims=True)
        dxh[r, :] = g1c * g1
        g2c = dot(gg[r, :], wupT[...])
        sm[3:4, :] += jnp.sum(g2c * xhb, axis=0, keepdims=True)
        sm[4:5, :] += jnp.sum(g2c, axis=0, keepdims=True)
        dxh[r, :] += g2c * g2
        rsd.give(i)
        if i == 1:
            ard.back(2)
            aru.back(2)

    small = {}

    def small_send(ax, n, src, buf, slot):
        buf[slot] = src
        for k in range(1, n):
            small[ax, k] = send(buf.at[slot], buf.at[slot], (ax, k))

    def small_sum(ax, n, buf):
        for k in range(1, n):
            small[ax, k].wait_recv()
        tot = buf[0]
        for k in range(1, n):
            tot = tot + buf[k]
        return tot

    small_send("y", 4, sm[...], smy, y)
    arw.step1(0)
    arw.step1(1)
    rsa.fold()
    ard.back(1)
    aru.back(1)
    arw.step2(0)
    arw.step2(1)
    rsd.fold()
    small_send("z", 4, small_sum("y", 4, smy), smz, z)
    arw.step3(0)
    arw.step3(1)
    rsa.second()
    rsd.second()
    tot_dp = small_sum("z", 4, smz)
    sm_out[5:6, :] = tot_dp[5:6]
    small_send("t", 8, tot_dp, smt, tn)
    ard.back(0)
    move(od, od_out)
    aru.back(0)
    move(ou, ou_out)

    out_b = row_of(ob_ref)
    for half in range(2):
        hr = pl.ds(half * 64, 64)
        hb = hidf[pl.ds(pl.multiple_of(own + half * 64, 64), 64), :].astype(f32)
        act_out[hr, :] = (hb + rsa.result(half) + out_b).astype(bf16)
    for half in range(2):
        hr = pl.ds(half * 64, 64)
        fr = pl.ds(pl.multiple_of(own + half * 64, 64), 64)
        d = rsd.result(half)
        xhat, rstd = norm_stats(hidf[fr, :].astype(f32))
        back = (d - jnp.mean(d, axis=1, keepdims=True) - xhat * jnp.mean(d * xhat, axis=1, keepdims=True)) * rstd
        ing_out[hr, :] = cotf[fr, :].astype(f32) + back
    sm_out[0:5, :] = small_sum("t", 8, smt)[0:5]
    sm_out[6:8, :] = jnp.zeros((2, D), f32)
    arw.finish(0)
    arw.finish(1)
    move(ow, ow_out)
    for cp in pending:
        cp.wait_send()
    for cp in moves[-3:]:
        cp.wait()


def layer(*args):
    v = lambda s, d: pltpu.VMEM(s, d)
    big = (1024, 1024)
    scratch = [
        v(big, bf16), v(big, bf16), v(big, bf16), v(big, bf16), v(big, bf16),
        v((1024, F), bf16), v((1024, F), f32), v((1024, F), bf16),
        v((1024, C), bf16), v((1024, C), bf16), v((1024, C), bf16), v((1024, C), bf16),
        v((C, 1024), bf16), v((C, 1024), bf16), v((C, 1024), bf16), v((1024, C), bf16),
        v((1024, 3 * C), bf16),
        v((1024, C), f32), v((1024, C), f32),
        v((3, 1024, C), bf16), v((C, D), bf16), v((D, F), bf16), v((F, D), bf16),
        v((1024, 3 * C), bf16), v((3 * C, 1024), bf16), v((F, 1024), bf16), v((1024, F), bf16), v((1024, C), bf16),
        v((1024, C), f32), v((1024, C), f32), v((1024, C), f32),
        v(big, f32), v(big, f32),
    ]
    for _ in range(2):
        scratch += [v((4, 256, F), bf16), v((4, 256, F), bf16), v((4, 256, F), bf16)]
    scratch += [
        v((4, 1024, C), bf16), v((2, 3, 2, 256, C), bf16), v((2, 2, 256, C), bf16), v((2, 3, 2, 64, C), bf16),
        v((4, 1024, C), bf16),
    ]
    for _ in range(2):
        scratch += [
            v((4, 128, D), bf16), v((4, 128, D), bf16), v((2, 2, 2, 64, D), bf16), v((2, 2, 64, D), bf16),
            v((2, 64, D), bf16),
        ]
    scratch += [v((8, D), f32), v((4, 8, D), f32), v((4, 8, D), f32), v((8, 8, D), f32)]
    scratch += [pltpu.SemaphoreType.DMA((NSEM,)), pltpu.SemaphoreType.DMA((NSEM,)), pltpu.SemaphoreType.DMA((12,))]
    vm = pl.BlockSpec(memory_space=pltpu.VMEM)
    hbm = pl.BlockSpec(memory_space=pl.ANY)
    return pl.pallas_call(
        kernel_body,
        out_shape=[
            jax.ShapeDtypeStruct((128, D), bf16),
            jax.ShapeDtypeStruct((128, D), f32),
            jax.ShapeDtypeStruct((4, 256, F), bf16),
            jax.ShapeDtypeStruct((4, 256, F), bf16),
            jax.ShapeDtypeStruct((4, 1024, C), bf16),
            jax.ShapeDtypeStruct((8, D), f32),
        ],
        in_specs=[hbm, hbm] + [vm] * 9 + [hbm] * 4,
        out_specs=[vm, vm, hbm, hbm, hbm, vm],
        scratch_shapes=scratch,
        compiler_params=pltpu.CompilerParams(
            collective_id=0, has_side_effects=True, vmem_limit_bytes=63 * 1024 * 1024
        ),
    )(*args)


def widen_body(
    act_ref, ing_ref, od_ref, ou_ref, ow_ref, sm_ref,
    act_out, ing_out, gq_out, gqb_out, gdn_out, gup_out, gub_out, gdown_out, ob_out, g1_out, b1_out, g2_out, b2_out,
    dbuf, ubuf, qbuf, nbuf, sem,
):
    copies = []

    def put(src, dst):
        cp = pltpu.make_async_copy(src, dst, sem.at[len(copies)])
        cp.start()
        copies.append(cp)

    put(act_ref, act_out.at[0])
    put(ing_ref, ing_out.at[0])
    for j in range(2):
        rows = pl.ds(j * 256, 256)
        for k in range(2):
            dbuf[rows, k * F:(k + 1) * F] = od_ref[2 * j + k].astype(f32)
        put(dbuf.at[rows], gdown_out.at[rows])
    for q in range(4):
        rows = pl.ds(q * 256, 256)
        ubuf[rows, :] = ou_ref[q].astype(f32)
        put(ubuf.at[rows], gup_out.at[rows])
    for i in range(3):
        qbuf[i] = ow_ref[i].astype(f32)
        put(qbuf.at[i], gq_out.at[i])
    for j in range(8):
        nbuf[:, j * C:(j + 1) * C] = ow_ref[3, j * C:(j + 1) * C, :].astype(f32)
    put(nbuf, gdn_out)
    gub_out[...] = sm_ref[5:6, 0:F]
    for i in range(3):
        gqb_out[i:i + 1, :] = sm_ref[5:6, F + i * C:F + (i + 1) * C]
    for i, ref in enumerate((ob_out, g1_out, b1_out, g2_out, b2_out)):
        ref[...] = sm_ref[i:i + 1, :]
    for cp in copies:
        cp.wait()


def widen(*args):
    vm = pl.BlockSpec(memory_space=pltpu.VMEM)
    hbm = pl.BlockSpec(memory_space=pl.ANY)
    one = jax.ShapeDtypeStruct((1, D), f32)
    return pl.pallas_call(
        widen_body,
        out_shape=[
            jax.ShapeDtypeStruct((1, 128, D), bf16),
            jax.ShapeDtypeStruct((1, 128, D), f32),
            jax.ShapeDtypeStruct((3, D, C), f32),
            jax.ShapeDtypeStruct((3, C), f32),
            jax.ShapeDtypeStruct((C, D), f32),
            jax.ShapeDtypeStruct((D, F), f32),
            jax.ShapeDtypeStruct((1, F), f32),
            jax.ShapeDtypeStruct((F, D), f32),
            one, one, one, one, one,
        ],
        in_specs=[hbm, hbm, vm, vm, vm, vm],
        out_specs=[hbm, hbm, hbm, vm, hbm, hbm, vm, hbm] + [vm] * 5,
        scratch_shapes=[
            pltpu.VMEM((F, D), f32), pltpu.VMEM((D, F), f32), pltpu.VMEM((3, D, C), f32), pltpu.VMEM((C, D), f32),
            pltpu.SemaphoreType.DMA((12,)),
        ],
        compiler_params=pltpu.CompilerParams(vmem_limit_bytes=63 * 1024 * 1024),
    )(*args)


def local(
    hidden_in, first_gain, first_shift, second_gain, second_shift, qkv_weight, qkv_bias, dense_weight,
    up_weight, up_bias, down_weight, out_bias, segments, positions, cotangent,
):
    parts = layer(
        hidden_in, cotangent, segments, positions, first_gain, first_shift, second_gain, second_shift, out_bias,
        up_bias, qkv_bias, qkv_weight, dense_weight, up_weight, down_weight,
    )
    act, ing, gq, gqb, gdn, gup, gub, gdown, ob, g1, b1, g2, b2 = widen(*parts)
    flat = lambda a: a.reshape(-1)
    return (act, ing, gq, gqb, gdn, gup, flat(gub), gdown, flat(ob), flat(g1), flat(b1), flat(g2), flat(b2))


def solution(mesh):
    placed = (
        P("dp", "tensor", None), P(), P(), P(), P(), P(None, None, "tensor"), P(None, "tensor"),
        P("tensor", None), P(None, "tensor"), P("tensor"), P("tensor", None), P(), P("dp", None),
        P("dp", None), P("dp", "tensor", None),
    )
    return jax.shard_map(
        local,
        mesh=mesh,
        in_specs=placed,
        out_specs=(
            P("dp", "tensor", None), P("dp", "tensor", None), P(None, None, "tensor"), P(None, "tensor"),
            P("tensor", None), P(None, "tensor"), P("tensor"), P("tensor", None), P(), P(), P(), P(), P(),
        ),
        check_vma=False,
    )
```

```python
import jax
import jax.numpy as jnp
from jax import lax
from jax.experimental import pallas as pl
from jax.experimental.pallas import tpu as pltpu
from jax.sharding import PartitionSpec as P

D = 1024
HD = 64
SEQ = 1024
F = 512
C = 128
EPS = 1e-05
f32 = jnp.float32
bf16 = jnp.bfloat16
NSEM = 176

YZ = ("yu", "yw", "zu", "zw")
ORD = tuple(tuple(YZ[(q + s) % 4] for s in range(4)) for q in range(4))


def dot(a, b):
    return lax.dot_general(a, b, (((1,), (0,)), ((), ())), preferred_element_type=f32)


def dot_nt(a, b):
    return lax.dot_general(a, b, (((1,), (1,)), ((), ())), preferred_element_type=f32)


def dot_tn(a, b):
    return lax.dot_general(a, b, (((0,), (0,)), ((), ())), preferred_element_type=f32)


def column(row, n):
    return jnp.broadcast_to(row.astype(f32), (n, row.shape[1])).T


def kernel_body(
    hid_ref, cot_ref, seg_ref, pos_ref, g1_ref, b1_ref, g2_ref, b2_ref, ob_ref, ub_ref, qb_ref,
    wqkv_ref, wd_ref, wup_ref, wdn_ref,
    act_out, ing_out, od_out, ou_out, ow_out, sm_out,
    hidf, cotf, xh, n1, n2, act_s, gel, gg, qs, ks, vs, ga, vT, kT, attT, att, gp,
    dk, dv, dqT, wqkv, wd, wup, wdn, wcat, wcatT, wupT, wdnT, wdT, ct, st, segc, po, dxh,
    gd, rd_, od, gu, ru_, ou, gw, rw1, pw, rw2, ow,
    sa, ra, ssa, r1a, r2a, sd, rd, ssd, r1d, r2d, sm, smy, smz, smt,
    ssem, rsem, lsem,
):
    dp = lax.axis_index("dp")
    tn = lax.axis_index("tensor")
    c = tn % 2
    x = tn // 2
    y = dp % 4
    z = dp // 4

    def flip(v):
        return v + 1 - 2 * (v % 2)

    def ub(v):
        return (v + v // 2) % 2

    def wb(v):
        return v // 2

    peer = {
        "c": (dp, x * 2 + 1 - c),
        "xu": (dp, flip(x) * 2 + c),
        "xw": (dp, (3 - x) * 2 + c),
        "yu": (z * 4 + flip(y), tn),
        "yw": (z * 4 + 3 - y, tn),
        "zu": (flip(z) * 4 + y, tn),
        "zw": ((3 - z) * 4 + y, tn),
    }
    ring = []
    for k in range(1, 4):
        peer["y", k] = (z * 4 + (y + k) % 4, tn)
        peer["z", k] = (((z + k) % 4) * 4 + y, tn)
        ring += [("y", k), ("z", k)]
    for k in range(1, 8):
        peer["t", k] = (dp, (tn + k) % 8)
        ring.append(("t", k))
    bit = {"yu": ub(y), "yw": wb(y), "zu": ub(z), "zw": wb(z)}
    xu, xw = ub(x), wb(x)

    pending = []
    count = [0]

    def send(src, dst, who):
        i = count[0]
        count[0] += 1
        cp = pltpu.make_async_remote_copy(
            src_ref=src, dst_ref=dst, send_sem=ssem.at[i], recv_sem=rsem.at[i],
            device_id=peer[who], device_id_type=pl.DeviceIdType.MESH,
        )
        cp.start()
        pending.append(cp)
        return cp

    own = pl.multiple_of(tn * 128, 128)
    own_rows = pl.ds(own, 128)
    moves = []

    def move(src, dst):
        cp = pltpu.make_async_copy(src, dst, lsem.at[len(moves)])
        cp.start()
        moves.append(cp)
        return cp

    m_hid = move(hid_ref.at[0], hidf.at[own_rows])
    m_cot = move(cot_ref.at[0], cotf.at[own_rows])
    m_w = [move(wqkv_ref, wqkv), move(wd_ref, wd), move(wup_ref, wup), move(wdn_ref, wdn)]

    barrier = pltpu.get_barrier_semaphore()
    for who in ring:
        pl.semaphore_signal(barrier, inc=1, device_id=peer[who], device_id_type=pl.DeviceIdType.MESH)
    pl.semaphore_wait(barrier, len(ring))

    x2 = flip(3 - x)
    tu = pl.multiple_of((flip(x) * 2 + c) * 128, 128)
    tw = pl.multiple_of(((3 - x) * 2 + c) * 128, 128)
    tuw = pl.multiple_of((x2 * 2 + c) * 128, 128)
    row_own = pl.multiple_of(x * 256, 256)
    row_u = pl.multiple_of(flip(x) * 256, 256)
    row_w = pl.multiple_of((3 - x) * 256, 256)
    row_uw = pl.multiple_of(x2 * 256, 256)

    class Gather:
        def __init__(self, src, full):
            self.src, self.full, self.cp = src, full, {}

        def fwd(self, i, row, n, who):
            ref = self.full.at[pl.ds(row, n)]
            self.cp[i] = send(ref, ref, who)

        def start_core(self):
            self.cp[0] = send(self.src.at[0], self.full.at[own_rows], "c")

        def start(self):
            lo, hi = self.src.at[0, pl.ds(0, 64)], self.src.at[0, pl.ds(64, 64)]
            dlo, dhi = self.full.at[pl.ds(own, 64)], self.full.at[pl.ds(own + 64, 64)]
            self.cp[1] = send(lo, dlo, "xu")
            self.cp[2] = send(hi, dhi, "xw")
            self.cp[3] = send(hi, dhi, "xu")
            self.cp[4] = send(lo, dlo, "xw")

        def mid(self):
            self.cp[1].wait_recv()
            self.fwd(5, tu, 64, "xw")
            self.cp[2].wait_recv()
            self.fwd(6, tw + 64, 64, "xu")

        def d2d(self):
            self.cp[3].wait_recv()
            self.fwd(7, tu, 128, "c")
            self.cp[4].wait_recv()
            self.fwd(8, tw, 128, "c")

        def last(self):
            self.cp[5].wait_recv()
            self.cp[6].wait_recv()
            self.fwd(9, tuw, 128, "c")

        def ready(self, i):
            self.cp[i].wait_recv()

    gh = Gather(hid_ref, hidf)
    gc = Gather(cot_ref, cotf)
    gh.start()
    gh.start_core()

    lane = lax.broadcasted_iota(jnp.int32, (1, C), 1)
    turn = lane % 8
    freq = jnp.zeros((1, C), f32)
    for j in range(8):
        freq = jnp.where(turn == j, 10000.0 ** (-2.0 * j / 16), freq)
    place = lane % HD
    freq = jnp.where(place < 16, freq, 0.0)
    sign = jnp.where(place < 8, -1.0, 1.0)
    low8 = place < 8

    @pl.loop(0, 8)
    def _(i):
        r = pl.ds(pl.multiple_of(i * 128, 128), 128)
        phase = column(pos_ref[0:1, r], 128) * freq
        ct[r, :] = jnp.cos(phase)
        st[r, :] = jnp.sin(phase) * sign
        segc[r, :] = column(seg_ref[0:1, r], 128)

    for cp in m_w:
        cp.wait()
    m_hid.wait()
    m_cot.wait()
    for i in range(3):
        wcat[:, i * C:(i + 1) * C] = wqkv[i]
        wcatT[i * C:(i + 1) * C, :] = wqkv[i].T

    gh.mid()
    gc.start()
    gc.start_core()

    wdT[...] = wd[...].T

    @pl.loop(0, 4)
    def _(i):
        r = pl.ds(pl.multiple_of(i * 128, 128), 128)
        wdnT[:, r] = wdn[r, :].T
        wupT[r, :] = wup[:, r].T

    def row_of(ref):
        return ref[...].astype(f32).reshape(1, -1)

    g1, b1, g2, b2 = row_of(g1_ref), row_of(b1_ref), row_of(g2_ref), row_of(b2_ref)
    up_b = row_of(ub_ref)
    qb_all = qb_ref[...].astype(f32)
    qkv_b = jnp.concatenate([qb_all[i:i + 1] for i in range(3)], axis=1)

    def partner(v):
        return jnp.where(low8, pltpu.roll(v, 120, 1), pltpu.roll(v, 8, 1))

    def norm_stats(xb):
        mu = jnp.mean(xb, axis=1, keepdims=True)
        xc = xb - mu
        rstd = lax.rsqrt(jnp.mean(xc * xc, axis=1, keepdims=True) + EPS)
        return xc * rstd, rstd

    def forward_rows(base):
        r = pl.ds(base, 256)
        xhat, _ = norm_stats(hidf[r, :].astype(f32))
        xh[r, :] = xhat.astype(bf16)
        m1 = (xhat * g1 + b1).astype(bf16)
        m2 = (xhat * g2 + b2).astype(bf16)
        n1[r, :] = m1
        n2[r, :] = m2
        gate = dot(m2, wup[...]) + up_b
        cdf = 0.5 * (1.0 + lax.erf(gate * 0.7071067811865476))
        act_s[r, :] = (gate * cdf).astype(bf16)
        gel[r, :] = cdf + gate * (jnp.exp(-0.5 * gate * gate) * 0.3989422804014327)
        pr = dot(m1, wcat[...]) + qkv_b
        cb, sb = ct[r, :], st[r, :]
        qp, kp, vp = pr[:, 0:C], pr[:, C:2 * C], pr[:, 2 * C:]
        qs[r, :] = ((qp * cb + partner(qp) * sb) * 0.125).astype(bf16)
        kr = kp * cb + partner(kp) * sb
        ks[r, :] = kr.astype(bf16)
        vs[r, :] = vp.astype(bf16)
        kT[:, r] = kr.T.astype(bf16)
        vT[:, r] = vp.T.astype(bf16)

    def backward_rows(base):
        r = pl.ds(base, 256)
        cb = cotf[r, :]
        gb = (dot(cb, wdnT[...]) * gel[r, :]).astype(bf16)
        gg[r, :] = gb
        sm[5:6, 0:F] += jnp.sum(gb.astype(f32), axis=0, keepdims=True)
        ga[r, :] = dot(cb, wdT[...]).astype(bf16)

    sm[...] = jnp.zeros((8, D), f32)
    sm[0:1, :] = jnp.sum(cotf[own_rows, :].astype(f32), axis=0, keepdims=True)

    gh.ready(0)
    forward_rows(row_own)
    gh.d2d()
    gh.ready(7)
    forward_rows(row_u)
    gh.last()
    gh.ready(8)
    forward_rows(row_w)
    gc.mid()
    gh.ready(9)
    forward_rows(row_uw)
    gc.d2d()
    gc.ready(0)
    backward_rows(row_own)
    gc.last()
    gc.ready(7)
    backward_rows(row_u)
    gc.ready(8)
    backward_rows(row_w)
    gc.ready(9)

    class AllReduce:
        def __init__(self, g, rr, o, n):
            self.g, self.r, self.o, self.n = g, rr, o, n
            self.off = {}
            self.cp = {}

        def rows(self, s):
            return self.n >> (s + 1)

        def start(self, s, qs_=range(4)):
            h = self.rows(s)
            for q in qs_:
                off = self.off[q, s] if s else 0
                b = bit[ORD[q][s]]
                self.off[q, s + 1] = pl.multiple_of(off + b * h, h)
                src = pl.multiple_of(off + (1 - b) * h, h)
                roff = self.n - 2 * h
                self.cp[q, s] = send(self.g.at[q, pl.ds(src, h)], self.r.at[q, pl.ds(roff, h)], ORD[q][s])

        def step(self, s):
            h = self.rows(s)
            roff = self.n - 2 * h
            for q in range(4):
                self.cp[q, s].wait_recv()
                keep = pl.ds(self.off[q, s + 1], h)
                tot = (self.g[q, keep, :].astype(f32) + self.r[q, pl.ds(roff, h), :].astype(f32)).astype(bf16)
                if s == 3:
                    self.o[q, keep, :] = tot
                    self.spread(3, (q,))
                else:
                    self.g[q, keep, :] = tot
                    self.start(s + 1, (q,))

        def spread(self, s, qs_=range(4)):
            h = self.rows(s)
            for q in qs_:
                ref = self.o.at[q, pl.ds(self.off[q, s + 1], h)]
                self.cp[q, 7 - s] = send(ref, ref, ORD[q][s])

        def back(self, s):
            for q in range(4):
                self.cp[q, 7 - s].wait_recv()
                if s > 0:
                    self.spread(s - 1, (q,))

    ard = AllReduce(gd, rd_, od, 256)
    aru = AllReduce(gu, ru_, ou, 256)

    for q in range(4):
        f0, d0 = 256 * (q // 2), 512 * (q % 2)
        gd[q] = dot_tn(act_s[:, f0:f0 + 256], cotf[:, d0:d0 + 512]).astype(bf16)
        ard.start(0, (q,))
    backward_rows(row_uw)
    for q in range(4):
        gu[q] = dot_tn(n2[:, 256 * q:256 * (q + 1)], gg[...]).astype(bf16)
        aru.start(0, (q,))

    dk[...] = jnp.zeros_like(dk)
    dv[...] = jnp.zeros_like(dv)

    def attention_half(i, h):
        q0, L = i * 256, (i + 1) * 256
        zero = jnp.zeros((), bf16)
        kidx = lax.broadcasted_iota(jnp.int32, (L, 256), 0)
        qidx = lax.broadcasted_iota(jnp.int32, (L, 256), 1) + q0
        sc = segc[0:L, :]
        same = jnp.concatenate([sc, sc], axis=1) == seg_ref[0:1, q0:L].astype(f32)
        allowed = same & (kidx <= qidx)
        mine = (lane // HD) == h
        qm, gm = jnp.where(mine, qs[q0:L, :], zero), jnp.where(mine, ga[q0:L, :], zero)
        s = jnp.where(allowed, dot_nt(ks[0:L, :], qm), -1e30)
        e = jnp.exp(s - jnp.max(s, axis=0, keepdims=True))
        p = e * (1.0 / jnp.sum(e, axis=0, keepdims=True))
        pb = p.astype(bf16)
        dp_ = dot_nt(vs[0:L, :], gm)
        ds = (p * (dp_ - jnp.sum(p * dp_, axis=0, keepdims=True))).astype(bf16)
        hr = slice(h * HD, (h + 1) * HD)
        attT[hr, q0:L] = dot(vT[hr, 0:L], pb).astype(bf16)
        dqT[hr, :] = dot(kT[hr, 0:L], ds)
        dv[0:L, :] += dot(pb, gm)
        dk[0:L, :] += dot(ds, qm)
        if h == 1:
            att[q0:L, :] = attT[:, q0:L].T
            cb, sb = ct[q0:L, :], st[q0:L, :]
            dq = dqT[...].T
            gp[q0:L, 0:C] = ((dq * cb - partner(dq) * sb) * 0.125).astype(bf16)
            dkb = dk[q0:L, :]
            gp[q0:L, C:2 * C] = (dkb * cb - partner(dkb) * sb).astype(bf16)
            gp[q0:L, 2 * C:] = dv[q0:L, :].astype(bf16)
            sm[5:6, F:F + 3 * C] += jnp.sum(gp[q0:L, :].astype(f32), axis=0, keepdims=True)

    attention_half(3, 0)
    attention_half(3, 1)
    ard.step(0)
    attention_half(2, 0)
    attention_half(2, 1)
    aru.step(0)
    attention_half(1, 0)
    ard.step(1)
    attention_half(1, 1)
    attention_half(0, 0)
    attention_half(0, 1)

    class RingReduce:
        def __init__(self):
            self.ax = (("y", y, "z", z), ("z", z, "y", y))
            self.cp = {}

        def start(self, a):
            ax, me, _, _ = self.ax[a]
            for k in (2, 1, 3):
                to = pl.multiple_of((me + k) % 4 * 256, 256)
                self.cp[a, 0, k] = send(gw.at[pl.ds(2 * a, 2), pl.ds(to, 256)], rw1.at[a, k - 1], (ax, k))

        def step1(self, a):
            _, me, ax, other = self.ax[a]
            for k in (1, 3, 2):
                self.cp[a, 0, k].wait_recv()
            tot = gw[pl.ds(2 * a, 2), pl.ds(pl.multiple_of(me * 256, 256), 256), :].astype(f32)
            for k in range(3):
                tot = tot + rw1[a, k].astype(f32)
            pw[a] = tot.astype(bf16)
            for k in (2, 1, 3):
                to = pl.multiple_of((other + k) % 4 * 64, 64)
                self.cp[a, 1, k] = send(pw.at[a, :, pl.ds(to, 64)], rw2.at[a, k - 1], (ax, k))

        def step2(self, a):
            _, me, ax, other = self.ax[a]
            for k in (1, 3, 2):
                self.cp[a, 1, k].wait_recv()
            tot = pw[a, :, pl.ds(pl.multiple_of(other * 64, 64), 64), :].astype(f32)
            for k in range(3):
                tot = tot + rw2[a, k].astype(f32)
            mine = pl.ds(pl.multiple_of(me * 256 + other * 64, 64), 64)
            ow[pl.ds(2 * a, 2), mine, :] = tot.astype(bf16)
            ref = ow.at[pl.ds(2 * a, 2), mine]
            for k in (2, 1, 3):
                self.cp[a, 2, k] = send(ref, ref, (ax, k))

        def step3(self, a):
            ax, me, _, _ = self.ax[a]
            for k in (1, 3, 2):
                self.cp[a, 2, k].wait_recv()
            ref = ow.at[pl.ds(2 * a, 2), pl.ds(pl.multiple_of(me * 256, 256), 256)]
            for k in (2, 1, 3):
                self.cp[a, 3, k] = send(ref, ref, (ax, k))

        def finish(self, a):
            for k in (1, 3, 2):
                self.cp[a, 3, k].wait_recv()

    arw = RingReduce()

    def attention_grads(i):
        r = slice(i * 256, (i + 1) * 256)
        res = dot_tn(n1[:, r], gp[...]).astype(bf16)
        gw[0, r, :] = res[:, 0:C]
        gw[1, r, :] = res[:, C:2 * C]
        gw[2, r, :] = res[:, 2 * C:]
        dn = dot(attT[...], cotf[:, r]).astype(bf16)
        gw[3, i * 256:i * 256 + 128, :] = dn[:, 0:C]
        gw[3, i * 256 + 128:i * 256 + 256, :] = dn[:, C:]

    attention_grads(0)
    aru.step(1)
    ard.step(2)
    attention_grads(1)
    attention_grads(2)
    attention_grads(3)
    arw.start(0)
    arw.start(1)
    aru.step(2)
    ard.step(3)

    class Scatter:
        def __init__(self, full, s0, r0, ss, r1, r2):
            self.full, self.s0, self.r0, self.ss, self.r1, self.r2 = full, s0, r0, ss, r1, r2
            self.cp = {}

        def give(self, i):
            row = pl.multiple_of(i * 256 + (1 - c) * 128, 128)
            self.s0[i] = self.full[pl.ds(row, 128), :].astype(bf16)
            self.cp[i] = send(self.s0.at[i], self.r0.at[i], "c")

        def fold(self):
            for u in range(2):
                for w in range(2):
                    i = 2 * w + (u ^ w)
                    self.cp[i].wait_recv()
                    row = pl.multiple_of(i * 256 + c * 128, 128)
                    val = (self.full[pl.ds(row, 128), :] + self.r0[i].astype(f32)).astype(bf16)
                    self.ss[0, u, w] = val[0:64]
                    self.ss[1, w, u] = val[64:128]
            self.cp[4] = send(self.ss.at[0, 1 - xu], self.r1.at[0], "xu")
            self.cp[5] = send(self.ss.at[1, 1 - xw], self.r1.at[1], "xw")

        def second(self):
            self.cp[4].wait_recv()
            for w in range(2):
                self.r1[0, w] = (self.r1[0, w].astype(f32) + self.ss[0, xu, w].astype(f32)).astype(bf16)
            self.cp[6] = send(self.r1.at[0, 1 - xw], self.r2.at[0], "xw")
            self.cp[5].wait_recv()
            for u in range(2):
                self.r1[1, u] = (self.r1[1, u].astype(f32) + self.ss[1, xw, u].astype(f32)).astype(bf16)
            self.cp[7] = send(self.r1.at[1, 1 - xu], self.r2.at[1], "xu")

        def result(self, half):
            self.cp[6 + half].wait_recv()
            mine = self.r1[0, xw] if half == 0 else self.r1[1, xu]
            return mine.astype(f32) + self.r2[half].astype(f32)

    rsa = Scatter(po, sa, ra, ssa, r1a, r2a)
    rsd = Scatter(dxh, sd, rd, ssd, r1d, r2d)

    for i in range(4):
        r = pl.ds(i * 256, 256)
        po[r, :] = dot(act_s[r, :], wdn[...]) + dot(att[r, :], wd[...])
        rsa.give(i)
    for i in range(4):
        r = pl.ds(i * 256, 256)
        xhb = xh[r, :].astype(f32)
        g1c = dot(gp[r, :], wcatT[...])
        sm[1:2, :] += jnp.sum(g1c * xhb, axis=0, keepdims=True)
        sm[2:3, :] += jnp.sum(g1c, axis=0, keepdims=True)
        dxh[r, :] = g1c * g1
        g2c = dot(gg[r, :], wupT[...])
        sm[3:4, :] += jnp.sum(g2c * xhb, axis=0, keepdims=True)
        sm[4:5, :] += jnp.sum(g2c, axis=0, keepdims=True)
        dxh[r, :] += g2c * g2
        rsd.give(i)
        if i == 1:
            rsa.fold()

    small = {}

    def small_send(ax, n, src, buf, slot):
        buf[slot] = src
        for k in range(1, n):
            small[ax, k] = send(buf.at[slot], buf.at[slot], (ax, k))

    def small_sum(ax, n, buf):
        for k in range(1, n):
            small[ax, k].wait_recv()
        tot = buf[0]
        for k in range(1, n):
            tot = tot + buf[k]
        return tot

    small_send("y", 4, sm[...], smy, y)
    arw.step1(0)
    arw.step1(1)
    aru.step(3)
    ard.back(3)
    rsd.fold()
    small_send("z", 4, small_sum("y", 4, smy), smz, z)
    arw.step2(0)
    arw.step2(1)
    aru.back(3)
    ard.back(2)
    tot_dp = small_sum("z", 4, smz)
    sm_out[5:6, :] = tot_dp[5:6]
    small_send("t", 8, tot_dp, smt, tn)
    rsa.second()
    arw.step3(0)
    arw.step3(1)
    aru.back(2)
    ard.back(1)
    rsd.second()
    aru.back(1)

    out_b = row_of(ob_ref)
    for half in range(2):
        hr = pl.ds(half * 64, 64)
        hb = hidf[pl.ds(pl.multiple_of(own + half * 64, 64), 64), :].astype(f32)
        act_out[hr, :] = (hb + rsa.result(half) + out_b).astype(bf16)
    ard.back(0)
    move(od, od_out)
    for half in range(2):
        hr = pl.ds(half * 64, 64)
        fr = pl.ds(pl.multiple_of(own + half * 64, 64), 64)
        d = rsd.result(half)
        xhat, rstd = norm_stats(hidf[fr, :].astype(f32))
        back = (d - jnp.mean(d, axis=1, keepdims=True) - xhat * jnp.mean(d * xhat, axis=1, keepdims=True)) * rstd
        ing_out[hr, :] = cotf[fr, :].astype(f32) + back
    sm_out[0:5, :] = small_sum("t", 8, smt)[0:5]
    sm_out[6:8, :] = jnp.zeros((2, D), f32)
    aru.back(0)
    move(ou, ou_out)
    arw.finish(0)
    arw.finish(1)
    move(ow, ow_out)
    for cp in pending:
        cp.wait_send()
    for cp in moves[-3:]:
        cp.wait()


def layer(*args):
    v = lambda s, d: pltpu.VMEM(s, d)
    big = (1024, 1024)
    scratch = [
        v(big, bf16), v(big, bf16), v(big, bf16), v(big, bf16), v(big, bf16),
        v((1024, F), bf16), v((1024, F), f32), v((1024, F), bf16),
        v((1024, C), bf16), v((1024, C), bf16), v((1024, C), bf16), v((1024, C), bf16),
        v((C, 1024), bf16), v((C, 1024), bf16), v((C, 1024), bf16), v((1024, C), bf16),
        v((1024, 3 * C), bf16),
        v((1024, C), f32), v((1024, C), f32), v((C, 256), f32),
        v((3, 1024, C), bf16), v((C, D), bf16), v((D, F), bf16), v((F, D), bf16),
        v((1024, 3 * C), bf16), v((3 * C, 1024), bf16), v((F, 1024), bf16), v((1024, F), bf16), v((1024, C), bf16),
        v((1024, C), f32), v((1024, C), f32), v((1024, C), f32),
        v(big, f32), v(big, f32),
    ]
    for _ in range(2):
        scratch += [v((4, 256, F), bf16), v((4, 256, F), bf16), v((4, 256, F), bf16)]
    scratch += [
        v((4, 1024, C), bf16), v((2, 3, 2, 256, C), bf16), v((2, 2, 256, C), bf16), v((2, 3, 2, 64, C), bf16),
        v((4, 1024, C), bf16),
    ]
    for _ in range(2):
        scratch += [
            v((4, 128, D), bf16), v((4, 128, D), bf16), v((2, 2, 2, 64, D), bf16), v((2, 2, 64, D), bf16),
            v((2, 64, D), bf16),
        ]
    scratch += [v((8, D), f32), v((4, 8, D), f32), v((4, 8, D), f32), v((8, 8, D), f32)]
    scratch += [pltpu.SemaphoreType.DMA((NSEM,)), pltpu.SemaphoreType.DMA((NSEM,)), pltpu.SemaphoreType.DMA((12,))]
    vm = pl.BlockSpec(memory_space=pltpu.VMEM)
    hbm = pl.BlockSpec(memory_space=pl.ANY)
    return pl.pallas_call(
        kernel_body,
        out_shape=[
            jax.ShapeDtypeStruct((128, D), bf16),
            jax.ShapeDtypeStruct((128, D), f32),
            jax.ShapeDtypeStruct((4, 256, F), bf16),
            jax.ShapeDtypeStruct((4, 256, F), bf16),
            jax.ShapeDtypeStruct((4, 1024, C), bf16),
            jax.ShapeDtypeStruct((8, D), f32),
        ],
        in_specs=[hbm, hbm] + [vm] * 9 + [hbm] * 4,
        out_specs=[vm, vm, hbm, hbm, hbm, vm],
        scratch_shapes=scratch,
        compiler_params=pltpu.CompilerParams(
            collective_id=0, has_side_effects=True, vmem_limit_bytes=63 * 1024 * 1024
        ),
    )(*args)


def widen_body(
    act_ref, ing_ref, od_ref, ou_ref, ow_ref, sm_ref,
    act_out, ing_out, gq_out, gqb_out, gdn_out, gup_out, gub_out, gdown_out, ob_out, g1_out, b1_out, g2_out, b2_out,
    act_v, ing_v, od_v, ou_v, ow_v, dbuf, ubuf, qbuf, nbuf, sem,
):
    copies = []

    def put(src, dst):
        cp = pltpu.make_async_copy(src, dst, sem.at[len(copies)])
        cp.start()
        copies.append(cp)
        return cp

    downs = [put(od_ref.at[pl.ds(2 * j, 2)], od_v.at[pl.ds(2 * j, 2)]) for j in range(2)]
    ups = [put(ou_ref.at[pl.ds(2 * j, 2)], ou_v.at[pl.ds(2 * j, 2)]) for j in range(2)]
    ows = put(ow_ref, ow_v)
    ings = put(ing_ref, ing_v)
    acts = put(act_ref, act_v)
    outs = []
    for j in range(2):
        rows = pl.ds(j * 256, 256)
        downs[j].wait()
        for k in range(2):
            dbuf[rows, k * F:(k + 1) * F] = od_v[2 * j + k].astype(f32)
        outs.append(put(dbuf.at[rows], gdown_out.at[rows]))
    for q in range(4):
        rows = pl.ds(q * 256, 256)
        if q % 2 == 0:
            ups[q // 2].wait()
        ubuf[rows, :] = ou_v[q].astype(f32)
        outs.append(put(ubuf.at[rows], gup_out.at[rows]))
    ows.wait()
    for i in range(3):
        qbuf[i] = ow_v[i].astype(f32)
        outs.append(put(qbuf.at[i], gq_out.at[i]))
    for j in range(8):
        nbuf[:, j * C:(j + 1) * C] = ow_v[3, j * C:(j + 1) * C, :].astype(f32)
    outs.append(put(nbuf, gdn_out))
    ings.wait()
    outs.append(put(ing_v, ing_out.at[0]))
    acts.wait()
    outs.append(put(act_v, act_out.at[0]))
    gub_out[...] = sm_ref[5:6, 0:F]
    for i in range(3):
        gqb_out[i:i + 1, :] = sm_ref[5:6, F + i * C:F + (i + 1) * C]
    for i, ref in enumerate((ob_out, g1_out, b1_out, g2_out, b2_out)):
        ref[...] = sm_ref[i:i + 1, :]
    for cp in outs:
        cp.wait()


def widen(*args):
    vm = pl.BlockSpec(memory_space=pltpu.VMEM)
    hbm = pl.BlockSpec(memory_space=pl.ANY)
    one = jax.ShapeDtypeStruct((1, D), f32)
    return pl.pallas_call(
        widen_body,
        out_shape=[
            jax.ShapeDtypeStruct((1, 128, D), bf16),
            jax.ShapeDtypeStruct((1, 128, D), f32),
            jax.ShapeDtypeStruct((3, D, C), f32),
            jax.ShapeDtypeStruct((3, C), f32),
            jax.ShapeDtypeStruct((C, D), f32),
            jax.ShapeDtypeStruct((D, F), f32),
            jax.ShapeDtypeStruct((1, F), f32),
            jax.ShapeDtypeStruct((F, D), f32),
            one, one, one, one, one,
        ],
        in_specs=[hbm] * 5 + [vm],
        out_specs=[hbm, hbm, hbm, vm, hbm, hbm, vm, hbm] + [vm] * 5,
        scratch_shapes=[
            pltpu.VMEM((128, D), bf16), pltpu.VMEM((128, D), f32), pltpu.VMEM((4, 256, F), bf16),
            pltpu.VMEM((4, 256, F), bf16), pltpu.VMEM((4, 1024, C), bf16),
            pltpu.VMEM((F, D), f32), pltpu.VMEM((D, F), f32), pltpu.VMEM((3, D, C), f32), pltpu.VMEM((C, D), f32),
            pltpu.SemaphoreType.DMA((24,)),
        ],
        compiler_params=pltpu.CompilerParams(vmem_limit_bytes=63 * 1024 * 1024),
    )(*args)


def local(
    hidden_in, first_gain, first_shift, second_gain, second_shift, qkv_weight, qkv_bias, dense_weight,
    up_weight, up_bias, down_weight, out_bias, segments, positions, cotangent,
):
    parts = layer(
        hidden_in, cotangent, segments, positions, first_gain, first_shift, second_gain, second_shift, out_bias,
        up_bias, qkv_bias, qkv_weight, dense_weight, up_weight, down_weight,
    )
    act, ing, gq, gqb, gdn, gup, gub, gdown, ob, g1, b1, g2, b2 = widen(*parts)
    flat = lambda a: a.reshape(-1)
    return (act, ing, gq, gqb, gdn, gup, flat(gub), gdown, flat(ob), flat(g1), flat(b1), flat(g2), flat(b2))


def solution(mesh):
    placed = (
        P("dp", "tensor", None), P(), P(), P(), P(), P(None, None, "tensor"), P(None, "tensor"),
        P("tensor", None), P(None, "tensor"), P("tensor"), P("tensor", None), P(), P("dp", None),
        P("dp", None), P("dp", "tensor", None),
    )
    return jax.shard_map(
        local,
        mesh=mesh,
        in_specs=placed,
        out_specs=(
            P("dp", "tensor", None), P("dp", "tensor", None), P(None, None, "tensor"), P(None, "tensor"),
            P("tensor", None), P(None, "tensor"), P("tensor"), P("tensor", None), P(), P(), P(), P(), P(),
        ),
        check_vma=False,
    )
```

```python
import jax
import jax.numpy as jnp
from jax import lax
from jax.experimental import pallas as pl
from jax.experimental.pallas import tpu as pltpu
from jax.sharding import PartitionSpec as P

D = 1024
HD = 64
SEQ = 1024
F = 512
C = 128
EPS = 1e-05
f32 = jnp.float32
bf16 = jnp.bfloat16
NSEM = 176

YZ = ("yu", "yw", "zu", "zw")
ORD = tuple(tuple(YZ[(q + s) % 4] for s in range(4)) for q in range(4))


def dot(a, b):
    return lax.dot_general(a, b, (((1,), (0,)), ((), ())), preferred_element_type=f32)


def dot_nt(a, b):
    return lax.dot_general(a, b, (((1,), (1,)), ((), ())), preferred_element_type=f32)


def dot_tn(a, b):
    return lax.dot_general(a, b, (((0,), (0,)), ((), ())), preferred_element_type=f32)


def column(row, n):
    return jnp.broadcast_to(row.astype(f32), (n, row.shape[1])).T


def kernel_body(
    hid_ref, cot_ref, seg_ref, pos_ref, g1_ref, b1_ref, g2_ref, b2_ref, ob_ref, ub_ref, qb_ref,
    wqkv_ref, wd_ref, wup_ref, wdn_ref,
    act_out, ing_out, od_out, ou_out, ow_out, sm_out,
    hidf, cotf, xh, n1, n2, act_s, gel, gg, qs, ks, vs, ga, vT, kT, attT, att, gp,
    dk, dv, dqT, wqkv, wd, wup, wdn, wcat, wcatT, wupT, wdnT, wdT, ct, st, segc, po, dxh,
    gd, rd_, od, gu, ru_, ou, gw, rw, ow,
    sa, ra, ssa, r1a, r2a, sd, rd, ssd, r1d, r2d, sm, smy, smz, smt, act_v, ing_v, sm_v,
    ssem, rsem, lsem,
):
    dp = lax.axis_index("dp")
    tn = lax.axis_index("tensor")
    c = tn % 2
    x = tn // 2
    y = dp % 4
    z = dp // 4

    def flip(v):
        return v + 1 - 2 * (v % 2)

    def ub(v):
        return (v + v // 2) % 2

    def wb(v):
        return v // 2

    peer = {
        "c": (dp, x * 2 + 1 - c),
        "xu": (dp, flip(x) * 2 + c),
        "xw": (dp, (3 - x) * 2 + c),
        "yu": (z * 4 + flip(y), tn),
        "yw": (z * 4 + 3 - y, tn),
        "zu": (flip(z) * 4 + y, tn),
        "zw": ((3 - z) * 4 + y, tn),
    }
    ring = []
    for k in range(1, 4):
        peer["y", k] = (z * 4 + (y + k) % 4, tn)
        peer["z", k] = (((z + k) % 4) * 4 + y, tn)
        ring += [("y", k), ("z", k)]
    for k in range(1, 8):
        peer["t", k] = (dp, (tn + k) % 8)
        ring.append(("t", k))
    bit = {"yu": ub(y), "yw": wb(y), "zu": ub(z), "zw": wb(z)}
    xu, xw = ub(x), wb(x)

    pending = []
    count = [0]

    def send(src, dst, who):
        i = count[0]
        count[0] += 1
        cp = pltpu.make_async_remote_copy(
            src_ref=src, dst_ref=dst, send_sem=ssem.at[i], recv_sem=rsem.at[i],
            device_id=peer[who], device_id_type=pl.DeviceIdType.MESH,
        )
        cp.start()
        pending.append(cp)
        return cp

    own = pl.multiple_of(tn * 128, 128)
    own_rows = pl.ds(own, 128)
    moves = []

    def move(src, dst):
        cp = pltpu.make_async_copy(src, dst, lsem.at[len(moves)])
        cp.start()
        moves.append(cp)
        return cp

    m_hid = move(hid_ref.at[0], hidf.at[own_rows])
    m_cot = move(cot_ref.at[0], cotf.at[own_rows])
    m_w = [move(wqkv_ref, wqkv), move(wd_ref, wd), move(wup_ref, wup), move(wdn_ref, wdn)]

    barrier = pltpu.get_barrier_semaphore()
    for who in ring:
        pl.semaphore_signal(barrier, inc=1, device_id=peer[who], device_id_type=pl.DeviceIdType.MESH)
    pl.semaphore_wait(barrier, len(ring))

    x2 = flip(3 - x)
    tu = pl.multiple_of((flip(x) * 2 + c) * 128, 128)
    tw = pl.multiple_of(((3 - x) * 2 + c) * 128, 128)
    tuw = pl.multiple_of((x2 * 2 + c) * 128, 128)
    row_own = pl.multiple_of(x * 256, 256)
    row_u = pl.multiple_of(flip(x) * 256, 256)
    row_w = pl.multiple_of((3 - x) * 256, 256)
    row_uw = pl.multiple_of(x2 * 256, 256)

    class Gather:
        def __init__(self, src, full):
            self.src, self.full, self.cp = src, full, {}

        def fwd(self, i, row, n, who):
            ref = self.full.at[pl.ds(row, n)]
            self.cp[i] = send(ref, ref, who)

        def start_core(self):
            self.cp[0] = send(self.src.at[0], self.full.at[own_rows], "c")

        def start(self):
            lo, hi = self.src.at[0, pl.ds(0, 64)], self.src.at[0, pl.ds(64, 64)]
            dlo, dhi = self.full.at[pl.ds(own, 64)], self.full.at[pl.ds(own + 64, 64)]
            self.cp[1] = send(lo, dlo, "xu")
            self.cp[2] = send(hi, dhi, "xw")
            self.cp[3] = send(hi, dhi, "xu")
            self.cp[4] = send(lo, dlo, "xw")

        def mid(self):
            self.cp[1].wait_recv()
            self.fwd(5, tu, 64, "xw")
            self.cp[2].wait_recv()
            self.fwd(6, tw + 64, 64, "xu")

        def d2d(self):
            self.cp[3].wait_recv()
            self.fwd(7, tu, 128, "c")
            self.cp[4].wait_recv()
            self.fwd(8, tw, 128, "c")

        def last(self):
            self.cp[5].wait_recv()
            self.cp[6].wait_recv()
            self.fwd(9, tuw, 128, "c")

        def ready(self, i):
            self.cp[i].wait_recv()

    gh = Gather(hid_ref, hidf)
    gc = Gather(cot_ref, cotf)
    gh.start()
    gh.start_core()

    lane = lax.broadcasted_iota(jnp.int32, (1, C), 1)
    turn = lane % 8
    freq = jnp.zeros((1, C), f32)
    for j in range(8):
        freq = jnp.where(turn == j, 10000.0 ** (-2.0 * j / 16), freq)
    place = lane % HD
    freq = jnp.where(place < 16, freq, 0.0)
    sign = jnp.where(place < 8, -1.0, 1.0)
    low8 = place < 8

    @pl.loop(0, 8)
    def _(i):
        r = pl.ds(pl.multiple_of(i * 128, 128), 128)
        phase = column(pos_ref[0:1, r], 128) * freq
        ct[r, :] = jnp.cos(phase)
        st[r, :] = jnp.sin(phase) * sign
        segc[r, :] = column(seg_ref[0:1, r], 128)

    for cp in m_w:
        cp.wait()
    m_hid.wait()
    m_cot.wait()
    for i in range(3):
        wcat[:, i * C:(i + 1) * C] = wqkv[i]
        wcatT[i * C:(i + 1) * C, :] = wqkv[i].T

    gh.mid()
    gc.start()
    gc.start_core()

    wdT[...] = wd[...].T

    @pl.loop(0, 4)
    def _(i):
        r = pl.ds(pl.multiple_of(i * 128, 128), 128)
        wdnT[:, r] = wdn[r, :].T
        wupT[r, :] = wup[:, r].T

    def row_of(ref):
        return ref[...].astype(f32).reshape(1, -1)

    g1, b1, g2, b2 = row_of(g1_ref), row_of(b1_ref), row_of(g2_ref), row_of(b2_ref)
    up_b = row_of(ub_ref)
    qb_all = qb_ref[...].astype(f32)
    qkv_b = jnp.concatenate([qb_all[i:i + 1] for i in range(3)], axis=1)

    def partner(v):
        return jnp.where(low8, pltpu.roll(v, 120, 1), pltpu.roll(v, 8, 1))

    def norm_stats(xb):
        mu = jnp.mean(xb, axis=1, keepdims=True)
        xc = xb - mu
        rstd = lax.rsqrt(jnp.mean(xc * xc, axis=1, keepdims=True) + EPS)
        return xc * rstd, rstd

    def forward_rows(base):
        r = pl.ds(base, 256)
        xhat, _ = norm_stats(hidf[r, :].astype(f32))
        xh[r, :] = xhat.astype(bf16)
        m1 = (xhat * g1 + b1).astype(bf16)
        m2 = (xhat * g2 + b2).astype(bf16)
        n1[r, :] = m1
        n2[r, :] = m2
        gate = dot(m2, wup[...]) + up_b
        cdf = 0.5 * (1.0 + lax.erf(gate * 0.7071067811865476))
        act_s[r, :] = (gate * cdf).astype(bf16)
        gel[r, :] = cdf + gate * (jnp.exp(-0.5 * gate * gate) * 0.3989422804014327)
        pr = dot(m1, wcat[...]) + qkv_b
        cb, sb = ct[r, :], st[r, :]
        qp, kp, vp = pr[:, 0:C], pr[:, C:2 * C], pr[:, 2 * C:]
        qs[r, :] = ((qp * cb + partner(qp) * sb) * 0.125).astype(bf16)
        kr = kp * cb + partner(kp) * sb
        ks[r, :] = kr.astype(bf16)
        vs[r, :] = vp.astype(bf16)
        kT[:, r] = kr.T.astype(bf16)
        vT[:, r] = vp.T.astype(bf16)

    def backward_rows(base):
        r = pl.ds(base, 256)
        cb = cotf[r, :]
        gb = (dot(cb, wdnT[...]) * gel[r, :]).astype(bf16)
        gg[r, :] = gb
        sm[5:6, 0:F] += jnp.sum(gb.astype(f32), axis=0, keepdims=True)
        ga[r, :] = dot(cb, wdT[...]).astype(bf16)

    sm[...] = jnp.zeros((8, D), f32)
    sm[0:1, :] = jnp.sum(cotf[own_rows, :].astype(f32), axis=0, keepdims=True)

    gh.ready(0)
    forward_rows(row_own)
    gh.d2d()
    gh.ready(7)
    forward_rows(row_u)
    gh.last()
    gh.ready(8)
    forward_rows(row_w)
    gc.mid()
    gh.ready(9)
    forward_rows(row_uw)
    gc.d2d()
    gc.ready(0)
    backward_rows(row_own)
    gc.last()
    gc.ready(7)
    backward_rows(row_u)
    gc.ready(8)
    backward_rows(row_w)
    gc.ready(9)

    class AllReduce:
        def __init__(self, g, rr, o, n):
            self.g, self.r, self.o, self.n = g, rr, o, n
            self.off = {}
            self.cp = {}

        def rows(self, s):
            return self.n >> (s + 1)

        def start(self, s, qs_=range(4)):
            h = self.rows(s)
            for q in qs_:
                off = self.off[q, s] if s else 0
                b = bit[ORD[q][s]]
                self.off[q, s + 1] = pl.multiple_of(off + b * h, h)
                src = pl.multiple_of(off + (1 - b) * h, h)
                roff = self.n - 2 * h
                self.cp[q, s] = send(self.g.at[q, pl.ds(src, h)], self.r.at[q, pl.ds(roff, h)], ORD[q][s])

        def step(self, s):
            h = self.rows(s)
            roff = self.n - 2 * h
            for q in range(4):
                self.cp[q, s].wait_recv()
                keep = pl.ds(self.off[q, s + 1], h)
                tot = (self.g[q, keep, :].astype(f32) + self.r[q, pl.ds(roff, h), :].astype(f32)).astype(bf16)
                if s == 3:
                    self.o[q, keep, :] = tot
                    self.spread(3, (q,))
                else:
                    self.g[q, keep, :] = tot
                    self.start(s + 1, (q,))

        def spread(self, s, qs_=range(4)):
            h = self.rows(s)
            for q in qs_:
                ref = self.o.at[q, pl.ds(self.off[q, s + 1], h)]
                self.cp[q, 7 - s] = send(ref, ref, ORD[q][s])

        def back(self, s):
            for q in range(4):
                self.cp[q, 7 - s].wait_recv()
                if s > 0:
                    self.spread(s - 1, (q,))

    ard = AllReduce(gd, rd_, od, 256)
    aru = AllReduce(gu, ru_, ou, 256)

    for q in range(4):
        f0, d0 = 256 * (q // 2), 512 * (q % 2)
        gd[q] = dot_tn(act_s[:, f0:f0 + 256], cotf[:, d0:d0 + 512]).astype(bf16)
        ard.start(0, (q,))
    backward_rows(row_uw)
    for q in range(4):
        gu[q] = dot_tn(n2[:, 256 * q:256 * (q + 1)], gg[...]).astype(bf16)
        aru.start(0, (q,))

    dk[...] = jnp.zeros_like(dk)
    dv[...] = jnp.zeros_like(dv)

    def attention_half(i, h):
        q0, L = i * 256, (i + 1) * 256
        zero = jnp.zeros((), bf16)
        kidx = lax.broadcasted_iota(jnp.int32, (L, 256), 0)
        qidx = lax.broadcasted_iota(jnp.int32, (L, 256), 1) + q0
        sc = segc[0:L, :]
        same = jnp.concatenate([sc, sc], axis=1) == seg_ref[0:1, q0:L].astype(f32)
        allowed = same & (kidx <= qidx)
        mine = (lane // HD) == h
        qm, gm = jnp.where(mine, qs[q0:L, :], zero), jnp.where(mine, ga[q0:L, :], zero)
        s = jnp.where(allowed, dot_nt(ks[0:L, :], qm), -1e30)
        e = jnp.exp(s - jnp.max(s, axis=0, keepdims=True))
        p = e * (1.0 / jnp.sum(e, axis=0, keepdims=True))
        pb = p.astype(bf16)
        dp_ = dot_nt(vs[0:L, :], gm)
        ds = (p * (dp_ - jnp.sum(p * dp_, axis=0, keepdims=True))).astype(bf16)
        hr = slice(h * HD, (h + 1) * HD)
        attT[hr, q0:L] = dot(vT[hr, 0:L], pb).astype(bf16)
        dqT[hr, :] = dot(kT[hr, 0:L], ds)
        dv[0:L, :] += dot(pb, gm)
        dk[0:L, :] += dot(ds, qm)
        if h == 1:
            att[q0:L, :] = attT[:, q0:L].T
            cb, sb = ct[q0:L, :], st[q0:L, :]
            dq = dqT[...].T
            gp[q0:L, 0:C] = ((dq * cb - partner(dq) * sb) * 0.125).astype(bf16)
            dkb = dk[q0:L, :]
            gp[q0:L, C:2 * C] = (dkb * cb - partner(dkb) * sb).astype(bf16)
            gp[q0:L, 2 * C:] = dv[q0:L, :].astype(bf16)
            sm[5:6, F:F + 3 * C] += jnp.sum(gp[q0:L, :].astype(f32), axis=0, keepdims=True)

    attention_half(3, 0)
    attention_half(3, 1)
    ard.step(0)
    attention_half(2, 0)
    attention_half(2, 1)
    aru.step(0)
    attention_half(1, 0)
    ard.step(1)
    attention_half(1, 1)
    attention_half(0, 0)
    attention_half(0, 1)

    arw = AllReduce(gw, rw, ow, 1024)

    def attention_grads(i):
        r = slice(i * 256, (i + 1) * 256)
        res = dot_tn(n1[:, r], gp[...]).astype(bf16)
        gw[0, r, :] = res[:, 0:C]
        gw[1, r, :] = res[:, C:2 * C]
        gw[2, r, :] = res[:, 2 * C:]
        dn = dot(attT[...], cotf[:, r]).astype(bf16)
        gw[3, i * 256:i * 256 + 128, :] = dn[:, 0:C]
        gw[3, i * 256 + 128:i * 256 + 256, :] = dn[:, C:]

    attention_grads(0)
    aru.step(1)
    ard.step(2)
    attention_grads(1)
    attention_grads(2)
    attention_grads(3)
    arw.start(0)
    aru.step(2)
    ard.step(3)

    class Scatter:
        def __init__(self, full, s0, r0, ss, r1, r2):
            self.full, self.s0, self.r0, self.ss, self.r1, self.r2 = full, s0, r0, ss, r1, r2
            self.cp = {}

        def give(self, i):
            row = pl.multiple_of(i * 256 + (1 - c) * 128, 128)
            self.s0[i] = self.full[pl.ds(row, 128), :].astype(bf16)
            self.cp[i] = send(self.s0.at[i], self.r0.at[i], "c")

        def fold(self):
            for u in range(2):
                for w in range(2):
                    i = 2 * w + (u ^ w)
                    self.cp[i].wait_recv()
                    row = pl.multiple_of(i * 256 + c * 128, 128)
                    val = (self.full[pl.ds(row, 128), :] + self.r0[i].astype(f32)).astype(bf16)
                    self.ss[0, u, w] = val[0:64]
                    self.ss[1, w, u] = val[64:128]
            self.cp[4] = send(self.ss.at[0, 1 - xu], self.r1.at[0], "xu")
            self.cp[5] = send(self.ss.at[1, 1 - xw], self.r1.at[1], "xw")

        def second(self):
            self.cp[4].wait_recv()
            for w in range(2):
                self.r1[0, w] = (self.r1[0, w].astype(f32) + self.ss[0, xu, w].astype(f32)).astype(bf16)
            self.cp[6] = send(self.r1.at[0, 1 - xw], self.r2.at[0], "xw")
            self.cp[5].wait_recv()
            for u in range(2):
                self.r1[1, u] = (self.r1[1, u].astype(f32) + self.ss[1, xw, u].astype(f32)).astype(bf16)
            self.cp[7] = send(self.r1.at[1, 1 - xu], self.r2.at[1], "xu")

        def result(self, half):
            self.cp[6 + half].wait_recv()
            mine = self.r1[0, xw] if half == 0 else self.r1[1, xu]
            return mine.astype(f32) + self.r2[half].astype(f32)

    rsa = Scatter(po, sa, ra, ssa, r1a, r2a)
    rsd = Scatter(dxh, sd, rd, ssd, r1d, r2d)

    for i in range(4):
        r = pl.ds(i * 256, 256)
        po[r, :] = dot(act_s[r, :], wdn[...]) + dot(att[r, :], wd[...])
        rsa.give(i)
    for i in range(4):
        r = pl.ds(i * 256, 256)
        xhb = xh[r, :].astype(f32)
        g1c = dot(gp[r, :], wcatT[...])
        sm[1:2, :] += jnp.sum(g1c * xhb, axis=0, keepdims=True)
        sm[2:3, :] += jnp.sum(g1c, axis=0, keepdims=True)
        dxh[r, :] = g1c * g1
        g2c = dot(gg[r, :], wupT[...])
        sm[3:4, :] += jnp.sum(g2c * xhb, axis=0, keepdims=True)
        sm[4:5, :] += jnp.sum(g2c, axis=0, keepdims=True)
        dxh[r, :] += g2c * g2
        rsd.give(i)
        if i == 1:
            arw.step(0)
            aru.step(3)
            ard.back(3)
            rsa.fold()

    small = {}

    def small_send(ax, n, src, buf, slot):
        buf[slot] = src
        for k in range(1, n):
            small[ax, k] = send(buf.at[slot], buf.at[slot], (ax, k))

    def small_sum(ax, n, buf):
        for k in range(1, n):
            small[ax, k].wait_recv()
        tot = buf[0]
        for k in range(1, n):
            tot = tot + buf[k]
        return tot

    small_send("y", 4, sm[...], smy, y)
    arw.step(1)
    aru.back(3)
    ard.back(2)
    rsd.fold()
    small_send("z", 4, small_sum("y", 4, smy), smz, z)
    arw.step(2)
    aru.back(2)
    rsa.second()
    arw.step(3)
    ard.back(1)
    tot_dp = small_sum("z", 4, smz)
    sm_v[5:6, :] = tot_dp[5:6]
    small_send("t", 8, tot_dp, smt, tn)
    arw.back(3)
    aru.back(1)
    sent = len(pending)
    arw.back(2)
    rsd.second()
    arw.back(1)
    for cp in pending[:sent]:
        cp.wait_send()

    out_b = row_of(ob_ref)
    for half in range(2):
        hr = pl.ds(half * 64, 64)
        hb = hidf[pl.ds(pl.multiple_of(own + half * 64, 64), 64), :].astype(f32)
        act_v[hr, :] = (hb + rsa.result(half) + out_b).astype(bf16)
    move(act_v, act_out)
    ard.back(0)
    move(od, od_out)
    for half in range(2):
        hr = pl.ds(half * 64, 64)
        fr = pl.ds(pl.multiple_of(own + half * 64, 64), 64)
        d = rsd.result(half)
        xhat, rstd = norm_stats(hidf[fr, :].astype(f32))
        back = (d - jnp.mean(d, axis=1, keepdims=True) - xhat * jnp.mean(d * xhat, axis=1, keepdims=True)) * rstd
        ing_v[hr, :] = cotf[fr, :].astype(f32) + back
    move(ing_v, ing_out)
    sm_v[0:5, :] = small_sum("t", 8, smt)[0:5]
    sm_v[6:8, :] = jnp.zeros((2, D), f32)
    move(sm_v, sm_out)
    aru.back(0)
    move(ou, ou_out)
    arw.back(0)
    move(ow, ow_out)
    for cp in pending[sent:]:
        cp.wait_send()
    for cp in moves[-6:]:
        cp.wait()


def layer(*args):
    v = lambda s, d: pltpu.VMEM(s, d)
    big = (1024, 1024)
    scratch = [
        v(big, bf16), v(big, bf16), v(big, bf16), v(big, bf16), v(big, bf16),
        v((1024, F), bf16), v((1024, F), f32), v((1024, F), bf16),
        v((1024, C), bf16), v((1024, C), bf16), v((1024, C), bf16), v((1024, C), bf16),
        v((C, 1024), bf16), v((C, 1024), bf16), v((C, 1024), bf16), v((1024, C), bf16),
        v((1024, 3 * C), bf16),
        v((1024, C), f32), v((1024, C), f32), v((C, 256), f32),
        v((3, 1024, C), bf16), v((C, D), bf16), v((D, F), bf16), v((F, D), bf16),
        v((1024, 3 * C), bf16), v((3 * C, 1024), bf16), v((F, 1024), bf16), v((1024, F), bf16), v((1024, C), bf16),
        v((1024, C), f32), v((1024, C), f32), v((1024, C), f32),
        v(big, f32), v(big, f32),
    ]
    for _ in range(2):
        scratch += [v((4, 256, F), bf16), v((4, 256, F), bf16), v((4, 256, F), bf16)]
    scratch += [
        v((4, 1024, C), bf16), v((4, 1024, C), bf16), v((4, 1024, C), bf16),
    ]
    for _ in range(2):
        scratch += [
            v((4, 128, D), bf16), v((4, 128, D), bf16), v((2, 2, 2, 64, D), bf16), v((2, 2, 64, D), bf16),
            v((2, 64, D), bf16),
        ]
    scratch += [v((8, D), f32), v((4, 8, D), f32), v((4, 8, D), f32), v((8, 8, D), f32)]
    scratch += [v((128, D), bf16), v((128, D), f32), v((8, D), f32)]
    scratch += [pltpu.SemaphoreType.DMA((NSEM,)), pltpu.SemaphoreType.DMA((NSEM,)), pltpu.SemaphoreType.DMA((12,))]
    vm = pl.BlockSpec(memory_space=pltpu.VMEM)
    hbm = pl.BlockSpec(memory_space=pl.ANY)
    return pl.pallas_call(
        kernel_body,
        out_shape=[
            jax.ShapeDtypeStruct((128, D), bf16),
            jax.ShapeDtypeStruct((128, D), f32),
            jax.ShapeDtypeStruct((4, 256, F), bf16),
            jax.ShapeDtypeStruct((4, 256, F), bf16),
            jax.ShapeDtypeStruct((4, 1024, C), bf16),
            jax.ShapeDtypeStruct((8, D), f32),
        ],
        in_specs=[hbm, hbm] + [vm] * 9 + [hbm] * 4,
        out_specs=[hbm] * 6,
        scratch_shapes=scratch,
        compiler_params=pltpu.CompilerParams(
            collective_id=0, has_side_effects=True, vmem_limit_bytes=63 * 1024 * 1024
        ),
    )(*args)


def widen_body(
    act_ref, ing_ref, od_ref, ou_ref, ow_ref, sm_ref,
    act_out, ing_out, gq_out, gqb_out, gdn_out, gup_out, gub_out, gdown_out, ob_out, g1_out, b1_out, g2_out, b2_out,
    act_v, ing_v, od_v, ou_v, ow_v, sm_v, dbuf, ubuf, qbuf, nbuf, rowb, upb, qkvb, sem,
):
    copies = []

    def put(src, dst):
        cp = pltpu.make_async_copy(src, dst, sem.at[len(copies)])
        cp.start()
        copies.append(cp)
        return cp

    downs = [put(od_ref.at[pl.ds(2 * j, 2)], od_v.at[pl.ds(2 * j, 2)]) for j in range(2)]
    ups = [put(ou_ref.at[pl.ds(2 * j, 2)], ou_v.at[pl.ds(2 * j, 2)]) for j in range(2)]
    ows = put(ow_ref, ow_v)
    ings = put(ing_ref, ing_v)
    acts = put(act_ref, act_v)
    sms = put(sm_ref, sm_v)
    outs = []
    for j in range(2):
        rows = pl.ds(j * 256, 256)
        downs[j].wait()
        for k in range(2):
            dbuf[rows, k * F:(k + 1) * F] = od_v[2 * j + k].astype(f32)
        outs.append(put(dbuf.at[rows], gdown_out.at[rows]))
    for q in range(4):
        rows = pl.ds(q * 256, 256)
        if q % 2 == 0:
            ups[q // 2].wait()
        ubuf[rows, :] = ou_v[q].astype(f32)
        outs.append(put(ubuf.at[rows], gup_out.at[rows]))
    ows.wait()
    for i in range(3):
        qbuf[i] = ow_v[i].astype(f32)
        outs.append(put(qbuf.at[i], gq_out.at[i]))
    for j in range(8):
        nbuf[:, j * C:(j + 1) * C] = ow_v[3, j * C:(j + 1) * C, :].astype(f32)
    outs.append(put(nbuf, gdn_out))
    ings.wait()
    outs.append(put(ing_v, ing_out.at[0]))
    acts.wait()
    outs.append(put(act_v, act_out.at[0]))
    sms.wait()
    upb[...] = sm_v[5:6, 0:F]
    outs.append(put(upb, gub_out))
    for i in range(3):
        qkvb[i:i + 1, :] = sm_v[5:6, F + i * C:F + (i + 1) * C]
    outs.append(put(qkvb, gqb_out))
    for i, ref in enumerate((ob_out, g1_out, b1_out, g2_out, b2_out)):
        rowb[i] = sm_v[i:i + 1, :]
        outs.append(put(rowb.at[i], ref))
    for cp in outs:
        cp.wait()


def widen(*args):
    hbm = pl.BlockSpec(memory_space=pl.ANY)
    one = jax.ShapeDtypeStruct((1, D), f32)
    return pl.pallas_call(
        widen_body,
        out_shape=[
            jax.ShapeDtypeStruct((1, 128, D), bf16),
            jax.ShapeDtypeStruct((1, 128, D), f32),
            jax.ShapeDtypeStruct((3, D, C), f32),
            jax.ShapeDtypeStruct((3, C), f32),
            jax.ShapeDtypeStruct((C, D), f32),
            jax.ShapeDtypeStruct((D, F), f32),
            jax.ShapeDtypeStruct((1, F), f32),
            jax.ShapeDtypeStruct((F, D), f32),
            one, one, one, one, one,
        ],
        in_specs=[hbm] * 6,
        out_specs=[hbm] * 13,
        scratch_shapes=[
            pltpu.VMEM((128, D), bf16), pltpu.VMEM((128, D), f32), pltpu.VMEM((4, 256, F), bf16),
            pltpu.VMEM((4, 256, F), bf16), pltpu.VMEM((4, 1024, C), bf16),
            pltpu.VMEM((8, D), f32),
            pltpu.VMEM((F, D), f32), pltpu.VMEM((D, F), f32), pltpu.VMEM((3, D, C), f32), pltpu.VMEM((C, D), f32),
            pltpu.VMEM((5, 1, D), f32), pltpu.VMEM((1, F), f32), pltpu.VMEM((3, C), f32),
            pltpu.SemaphoreType.DMA((32,)),
        ],
        compiler_params=pltpu.CompilerParams(vmem_limit_bytes=63 * 1024 * 1024),
    )(*args)


def local(
    hidden_in, first_gain, first_shift, second_gain, second_shift, qkv_weight, qkv_bias, dense_weight,
    up_weight, up_bias, down_weight, out_bias, segments, positions, cotangent,
):
    parts = layer(
        hidden_in, cotangent, segments, positions, first_gain, first_shift, second_gain, second_shift, out_bias,
        up_bias, qkv_bias, qkv_weight, dense_weight, up_weight, down_weight,
    )
    act, ing, gq, gqb, gdn, gup, gub, gdown, ob, g1, b1, g2, b2 = widen(*parts)
    flat = lambda a: a.reshape(-1)
    return (act, ing, gq, gqb, gdn, gup, flat(gub), gdown, flat(ob), flat(g1), flat(b1), flat(g2), flat(b2))


def solution(mesh):
    placed = (
        P("dp", "tensor", None), P(), P(), P(), P(), P(None, None, "tensor"), P(None, "tensor"),
        P("tensor", None), P(None, "tensor"), P("tensor"), P("tensor", None), P(), P("dp", None),
        P("dp", None), P("dp", "tensor", None),
    )
    return jax.shard_map(
        local,
        mesh=mesh,
        in_specs=placed,
        out_specs=(
            P("dp", "tensor", None), P("dp", "tensor", None), P(None, None, "tensor"), P(None, "tensor"),
            P("tensor", None), P(None, "tensor"), P("tensor"), P("tensor", None), P(), P(), P(), P(), P(),
        ),
        check_vma=False,
    )
```
